1024 devices in a mesh: pipe: 16 (over y_hi, x, core), expert: 32 (over z), dp: 2 (over y_lo).
Axes of the slice: x: 4, y: 4 (y_hi: 2, y_lo: 2; y = y_hi * 2 + y_lo), z: 32, core: 2. Of those that a mesh axis runs over, the one named last changes fastest.
Arguments:
- fwd_sent: bfloat16 [16, 512, 7168], P('pipe', 'dp', 'expert'), may hold values from -6 to 6
- fwd_route: int32 [16, 512, 1], P('pipe', 'dp'), may hold values from 0 to 1; in each aligned block of 256 rows (0 to 255, 256 to 511, ..., all dimensions but the last counted through in order) at most 144 rows name the same one
- fwd_weight: bfloat16 [16, 512, 1], P('pipe', 'dp'), may hold values from 0.099609375 to 1
- bwd_cot: bfloat16 [16, 512, 7168], P('pipe', 'dp', 'expert'), may hold values from -6 to 6
- bwd_route: int32 [16, 512, 1], P('pipe', 'dp'), may hold values from 0 to 1; in each aligned block of 256 rows (0 to 255, 256 to 511, ..., all dimensions but the last counted through in order) at most 144 rows name the same one
- bwd_weight: bfloat16 [16, 512, 1], P('pipe', 'dp'), may hold values from 0.099609375 to 1
- saved_gate: bfloat16 [16, 2, 144, 2048], P('pipe', 'dp', None, 'expert'), may hold values from -6 to 6
- saved_up: bfloat16 [16, 2, 144, 2048], P('pipe', 'dp', None, 'expert'), may hold values from -6 to 6
- gate_weight: bfloat16 [16, 2048, 7168], P('pipe', 'expert'), may hold values from -0.0625 to 0.0625
- up_weight: bfloat16 [16, 2048, 7168], P('pipe', 'expert'), may hold values from -0.0625 to 0.0625
- down_weight: bfloat16 [16, 2048, 7168], P('pipe', 'expert'), may hold values from -0.1875 to 0.1875
Outputs:
- fwd_out: bfloat16 [16, 512, 7168], P('pipe', 'dp', 'expert')
- bwd_grad: bfloat16 [16, 512, 7168], P('pipe', 'dp', 'expert')
- down_grad: float32 [16, 2048, 7168], P('pipe', ('expert', 'dp'))
The draws below stay inside these ranges and needn't reach their ends.
Inputs may be any that keep to these rules, and one draw needn't show every extreme that they name: `fwd_route`: each row names 1 different experts. In each aligned block of 256 rows (the rows of one replica of a section) no expert is named by more than 144 rows, a bound that some block reaches. `bwd_route`: each row names 1 different experts. In each aligned block of 256 rows (the rows of one replica of a section) no expert is named by more than 144 rows, a bound that some block reaches.
All inputs are finite; a program needn't handle non-finite values.
Results may differ from the reference program's by a relative error of at most 0.0049.
Values may be sent and summed in bfloat16 or wider, within the bound.
A program may use at most 64 MiB of HBM per device.

```python
import math
import jax
import jax.numpy as jnp
import numpy as np
from jax import lax

D = 7168
FF = 1024
EXPERTS = 2
TOPK = 1
ROWS = 256
SECTIONS = 16
REPLICAS = 2
TOKENS = 512
UNITS = 64
CAP = 144


def levels(own_key, shape, pieces, least, largest):
    def one(dim, blocks):
        draws = jax.random.uniform(jax.random.fold_in(jax.random.fold_in(own_key, 6), dim), (blocks,), jnp.float32, least / len(pieces), largest / len(pieces))
        return jnp.repeat(jnp.exp(draws), shape[dim] // blocks).reshape((-1,) + (1,) * (len(shape) - dim - 1))

    loudness = one(*pieces[0])
    for cut in pieces[1:]:
        loudness = loudness * one(*cut)
    return loudness


def routed_block(own_key, own, number, rows, amount, top, limit, lean):
    order = jax.random.permutation(own_key, amount)
    heavy_load, ordinary = shares(amount, rows * top, limit, lean, True), shares(amount, rows * top, limit, lean, False)
    places = jnp.arange(amount)

    def named(lengths, rotation):
        used = int((lengths > 0).sum())
        fixed = max(1, used // 4)
        passed = fixed + (places - fixed + rotation * (used - fixed)) % max(1, amount - fixed)
        return jnp.zeros((amount,), jnp.int32).at[order[jnp.where(places < fixed, places, passed)]].set(jnp.asarray(lengths, jnp.int32))

    lengths = jnp.where(number % 4 == 0, named(heavy_load, number // 4), named(ordinary, number - number // 4 - 1))
    mixed = jax.random.permutation(jax.random.fold_in(own, 3), amount)
    giver, sink = mixed[0:amount // 2 * 2:2], mixed[1:amount // 2 * 2:2]
    margin = jnp.minimum(lengths[giver] - 1, limit - lengths[sink]) // 2
    margin = jnp.where((giver == order[0]) | (sink == order[0]) | (lengths[sink] == 0), 0, jnp.maximum(margin, 0))
    passed = jax.random.randint(jax.random.fold_in(own, 4), (amount // 2,), 0, 1 << 20) % (margin + 1)
    lengths = lengths.at[giver].add(-passed).at[sink].add(passed)
    labels = jnp.searchsorted(jnp.cumsum(lengths), jnp.arange(rows * top), side="right").astype(jnp.int32)
    grid = labels.reshape(top, rows).T
    grid = grid[jax.random.permutation(jax.random.fold_in(own, 1), rows)]
    rotation = jax.random.randint(jax.random.fold_in(own, 2), (rows, 1), 0, top)
    return jnp.take_along_axis(grid, (jnp.arange(top)[None, :] + rotation) % top, axis=1)


def shares(count, total, limit, lean, full):
    portions = [(1 << 20) // math.isqrt(rank ** lean) + 1 for rank in range(1, count + 1)]
    largest = limit if full else min(limit, max(-(-total // count), total * portions[0] // sum(portions)))
    least = 1 if total - largest >= count - 1 else 0
    counts, rest = [largest] + [least] * (count - 1), total - largest - least * (count - 1)
    while rest > 0:
        free = [i for i in range(1, count) if counts[i] < largest] or [i for i in range(1, count) if counts[i] < limit]
        mass, left = sum([portions[i] for i in free]), rest
        for i in free:
            more = min(limit - counts[i], max(1, left * portions[i] // mass), rest)
            counts[i] = counts[i] + more
            rest = rest - more
    return np.array(counts)


def centred(own_key, dims, spread, limit, shards=(), held_as=jnp.bfloat16):
    array = spread * jax.random.normal(own_key, dims, jnp.float32)
    if shards:
        array = array * levels(own_key, dims, shards, -0.22, 0.18)
    return jnp.clip(array, -limit, limit).astype(held_as)


def setup_inputs(seed: int = 0) -> dict:
    splits = jax.random.split(jax.random.key(seed), 12)
    fwd_sent = centred(splits[0], (SECTIONS, TOKENS, D), 1.0, 6.0, ((0, 16), (1, 2), (2, 32)))
    fwd_route_keys = jax.random.split(jax.random.fold_in(splits[1], 1), SECTIONS * TOKENS // ROWS)
    fwd_route_turns = jax.random.permutation(jax.random.fold_in(splits[1], 3), SECTIONS * TOKENS // ROWS)
    fwd_route = jax.vmap(lambda own, number: routed_block(jax.random.fold_in(splits[1], 2), own, number, ROWS, EXPERTS, TOPK, CAP, 2))(fwd_route_keys, fwd_route_turns).reshape((SECTIONS, TOKENS, TOPK))
    fwd_weight = jnp.clip(0.099609375 + 0.9003906 * jax.random.uniform(splits[2], (SECTIONS, TOKENS, TOPK), jnp.float32) ** levels(splits[2], (SECTIONS, TOKENS, TOPK), ((0, 16), (1, 2)), -0.2, 0.2), 0.099609375, 1.0).astype(jnp.bfloat16)
    bwd_cot = centred(splits[3], (SECTIONS, TOKENS, D), 1.0, 6.0, ((0, 16), (1, 2), (2, 32)))
    bwd_route_keys = jax.random.split(jax.random.fold_in(splits[4], 1), SECTIONS * TOKENS // ROWS)
    bwd_route_turns = jax.random.permutation(jax.random.fold_in(splits[4], 3), SECTIONS * TOKENS // ROWS)
    bwd_route = jax.vmap(lambda own, number: routed_block(jax.random.fold_in(splits[4], 2), own, number, ROWS, EXPERTS, TOPK, CAP, 2))(bwd_route_keys, bwd_route_turns).reshape((SECTIONS, TOKENS, TOPK))
    bwd_weight = jnp.clip(0.099609375 + 0.9003906 * jax.random.uniform(splits[5], (SECTIONS, TOKENS, TOPK), jnp.float32) ** levels(splits[5], (SECTIONS, TOKENS, TOPK), ((0, 16), (1, 2)), -0.2, 0.2), 0.099609375, 1.0).astype(jnp.bfloat16)
    saved_gate = centred(splits[6], (SECTIONS, REPLICAS, CAP, EXPERTS * FF), 1.0, 6.0, ((0, 16), (1, 2), (3, 32)))
    saved_up = centred(splits[7], (SECTIONS, REPLICAS, CAP, EXPERTS * FF), 1.0, 6.0, ((0, 16), (1, 2), (3, 32)))
    gate_weight = centred(splits[8], (SECTIONS, EXPERTS * FF, D), D ** -0.5, 0.0625, ((0, 16), (1, 32)))
    up_weight = centred(splits[9], (SECTIONS, EXPERTS * FF, D), D ** -0.5, 0.0625, ((0, 16), (1, 32)))
    down_weight = centred(splits[10], (SECTIONS, EXPERTS * FF, D), FF ** -0.5, 0.1875, ((0, 16), (1, 32)))
    return {"fwd_sent": fwd_sent, "fwd_route": fwd_route, "fwd_weight": fwd_weight, "bwd_cot": bwd_cot, "bwd_route": bwd_route, "bwd_weight": bwd_weight, "saved_gate": saved_gate, "saved_up": saved_up, "gate_weight": gate_weight, "up_weight": up_weight, "down_weight": down_weight}


def layout(route, experts, capacity):
    tokens, topk = route.shape
    flat = route.reshape(tokens * topk)
    onehot = (flat[:, None] == jnp.arange(experts, dtype=jnp.int32)[None, :]).astype(jnp.int32)
    before = jnp.cumsum(onehot, axis=0) - onehot
    slot = jnp.sum(before * onehot, axis=1)
    target = flat * capacity + slot
    placed = (target[:, None] == jnp.arange(experts * capacity, dtype=jnp.int32)[None, :]).astype(jnp.float32)
    return placed.reshape(tokens, topk, experts * capacity)


def expert_forward(rows, w_gate, w_up, w_down, groups):
    contract = (((1,), (1,)), ((), ()))
    gate = lax.dot_general(rows, w_gate, contract, preferred_element_type=jnp.float32)
    upper = lax.dot_general(rows, w_up, contract, preferred_element_type=jnp.float32)
    hidden = (gate * jax.nn.sigmoid(gate) * upper).astype(jnp.bfloat16)
    width = rows.shape[1]
    units = hidden.shape[1] // groups
    parts = jnp.einsum("cgu,gud->gcd", hidden.reshape(-1, groups, units).astype(jnp.float32), w_down.reshape(groups, units, width).astype(jnp.float32), precision=lax.Precision.HIGHEST)
    rounded = lax.optimization_barrier(parts.astype(jnp.bfloat16)).astype(jnp.float32)
    return jnp.sum(rounded, axis=0).astype(jnp.bfloat16)


def expert_backward(cot_rows, gate_pre, up_pre, w_gate, w_up, w_down, groups):
    gate = gate_pre.astype(jnp.float32)
    upper = up_pre.astype(jnp.float32)
    sig = jax.nn.sigmoid(gate)
    hidden = (gate * sig * upper).astype(jnp.bfloat16)
    contract = (((1,), (1,)), ((), ()))
    d_hidden = lax.dot_general(cot_rows, w_down, contract, preferred_element_type=jnp.float32)
    d_gate = (d_hidden * upper * sig * (1.0 + gate * (1.0 - sig))).astype(jnp.bfloat16)
    d_up = (d_hidden * gate * sig).astype(jnp.bfloat16)
    width = w_gate.shape[1]
    units = d_gate.shape[1] // groups
    parts = jnp.einsum("cgu,gud->gcd", d_gate.reshape(-1, groups, units).astype(jnp.float32), w_gate.reshape(groups, units, width).astype(jnp.float32), precision=lax.Precision.HIGHEST)
    parts = parts + jnp.einsum("cgu,gud->gcd", d_up.reshape(-1, groups, units).astype(jnp.float32), w_up.reshape(groups, units, width).astype(jnp.float32), precision=lax.Precision.HIGHEST)
    rounded = lax.optimization_barrier(parts.astype(jnp.bfloat16)).astype(jnp.float32)
    return jnp.sum(rounded, axis=0).astype(jnp.bfloat16), hidden


def reference(fwd_sent, fwd_route, fwd_weight, bwd_cot, bwd_route, bwd_weight, saved_gate, saved_up, gate_weight, up_weight, down_weight):
    arrive = jnp.roll(fwd_sent, 1, axis=0)
    cotangent = jnp.roll(bwd_cot, -1, axis=0)
    groups = FF // UNITS

    def one_section(items):
        rows_f, route_f, weight_f, cot, route_b, weight_b, pre_gate, pre_up, w_gate, w_up, w_down = items
        fwd_blocks = []
        bwd_blocks = []
        grad_terms = []
        for block in range(REPLICAS):
            low = block * ROWS
            x_rows = rows_f[low:low + ROWS]
            c_rows = cot[low:low + ROWS]
            place_f = layout(route_f[low:low + ROWS], EXPERTS, CAP)
            place_b = layout(route_b[low:low + ROWS], EXPERTS, CAP)
            select_f = jnp.sum(place_f, axis=1).astype(jnp.bfloat16)
            mix_f = jnp.sum(weight_f[low:low + ROWS].astype(jnp.float32)[:, :, None] * place_f, axis=1).astype(jnp.bfloat16)
            scale_b = jnp.sum(weight_b[low:low + ROWS].astype(jnp.float32)[:, :, None] * place_b, axis=1).astype(jnp.bfloat16)
            ones_b = jnp.sum(place_b, axis=1).astype(jnp.bfloat16)
            buffer = jnp.dot(select_f.T, x_rows, preferred_element_type=jnp.float32).astype(jnp.bfloat16)
            cot_buffer = jnp.dot(scale_b.T, c_rows, preferred_element_type=jnp.float32).astype(jnp.bfloat16)
            outputs = []
            gradients = []
            terms = []
            for expert in range(EXPERTS):
                first = expert * FF
                start = expert * CAP
                outputs.append(expert_forward(buffer[start:start + CAP], w_gate[first:first + FF], w_up[first:first + FF], w_down[first:first + FF], groups))
                grad, hidden = expert_backward(cot_buffer[start:start + CAP], pre_gate[block, :, first:first + FF], pre_up[block, :, first:first + FF], w_gate[first:first + FF], w_up[first:first + FF], w_down[first:first + FF], groups)
                gradients.append(grad)
                terms.append(lax.dot_general(hidden, cot_buffer[start:start + CAP], (((0,), (0,)), ((), ())), preferred_element_type=jnp.float32))
            expert_out = jnp.concatenate(outputs, axis=0)
            expert_grad = jnp.concatenate(gradients, axis=0)
            fwd_blocks.append((x_rows.astype(jnp.float32) + jnp.dot(mix_f, expert_out, preferred_element_type=jnp.float32)).astype(jnp.bfloat16))
            bwd_blocks.append((c_rows.astype(jnp.float32) + jnp.dot(ones_b, expert_grad, preferred_element_type=jnp.float32)).astype(jnp.bfloat16))
            grad_terms.append(jnp.concatenate(terms, axis=0))
        down_grad = grad_terms[0]
        for extra in grad_terms[1:]:
            down_grad = down_grad + extra
        return jnp.concatenate(fwd_blocks, axis=0), jnp.concatenate(bwd_blocks, axis=0), down_grad

    return lax.map(one_section, (arrive, fwd_route, fwd_weight, cotangent, bwd_route, bwd_weight, saved_gate, saved_up, gate_weight, up_weight, down_weight))
```

```python
import functools

import jax
import jax.numpy as jnp
from jax import lax
from jax.experimental import pallas as pl
from jax.experimental.pallas import tpu as pltpu
from jax.sharding import PartitionSpec as P

EXPERTS = 2
LANES = 128
MESH = pl.DeviceIdType.MESH
BY_UNITS = (((1,), (1,)), ((), ()))
F32 = jnp.float32
BF16 = jnp.bfloat16


def dot(a, b):
    return jnp.dot(a, b, preferred_element_type=F32)


def dot_t(a, b):
    return lax.dot_general(a, b, BY_UNITS, preferred_element_type=F32)


def pack(main, tail, rest):
    quarter = tail.shape[0] // 4
    spare = LANES - rest
    lane = lax.broadcasted_iota(jnp.int32, (quarter, LANES), 1)
    last = tail[3 * quarter :]
    parts = [main]
    for k in range(3):
        moved = pltpu.roll(last, rest - spare * k, axis=1)
        parts.append(jnp.where(lane < rest, tail[k * quarter : (k + 1) * quarter], moved))
    return jnp.concatenate(parts, axis=0)


def unpack(packed, rows, rest):
    quarter = rows // 4
    spare = LANES - rest
    lane = lax.broadcasted_iota(jnp.int32, (quarter, LANES), 1)
    pieces = [packed[rows + k * quarter : rows + (k + 1) * quarter] for k in range(3)]
    last = pltpu.roll(pieces[2].astype(F32), LANES - rest + 2 * spare, axis=1)
    for k in (1, 0):
        moved = pltpu.roll(pieces[k].astype(F32), LANES - rest + k * spare, axis=1)
        last = jnp.where(lane < (k + 1) * spare, moved, last)
    tail = jnp.concatenate(pieces + [last.astype(packed.dtype)], axis=0)
    return packed[:rows], tail


def kernel(
    ring,
    sections,
    x_ref,
    froute_ref,
    fweight_ref,
    c_ref,
    broute_ref,
    bweight_ref,
    sgate_ref,
    sup_ref,
    wg_ref,
    wu_ref,
    wd_ref,
    fout_ref,
    bout_ref,
    dgrad_ref,
    xs,
    cs,
    craw,
    gath_f,
    gath_b,
    red_f,
    red_b,
    wgu,
    wdn,
    acc_f,
    acc_b,
    coef_g,
    coef_u,
    hbt,
    hid,
    dgu,
    dg,
    dg_in,
    pipe_send,
    pipe_recv,
    gs_f,
    gr_f,
    gs_b,
    gr_b,
    rs_f,
    rr_f,
    rs_b,
    rr_b,
    dp_send,
    dp_recv,
):
    rows, width = x_ref.shape
    units = wg_ref.shape[0]
    capacity = sgate_ref.shape[0]
    rest = width - LANES
    half = ring // 2
    quarter = rows // 4
    dense = rows + 3 * quarter
    me = lax.axis_index("expert")
    section = lax.axis_index("pipe")
    replica = lax.axis_index("dp")
    right, left = lax.rem(me + 1, ring), lax.rem(me + ring - 1, ring)
    ahead, behind = lax.rem(section + 1, sections), lax.rem(section + sections - 1, sections)
    peer = 1 - replica
    expert = me // (ring // EXPERTS)

    barrier = pltpu.get_barrier_semaphore()
    for axis, other in (
        ("expert", right),
        ("expert", left),
        ("pipe", ahead),
        ("pipe", behind),
        ("dp", peer),
    ):
        pl.semaphore_signal(barrier, inc=1, device_id={axis: other}, device_id_type=MESH)

    def to_dense(ref):
        value = ref[...].astype(F32)
        tail = jnp.concatenate([value[:, LANES:], jnp.zeros((rows, LANES - rest), F32)], axis=1)
        return pack(value[:, :LANES], tail, rest).astype(BF16)

    xs[...] = to_dense(x_ref)
    cs[...] = to_dense(c_ref)
    pl.semaphore_wait(barrier, 5)

    def shift(k):
        return pltpu.make_async_remote_copy(
            src_ref=(xs, cs)[k],
            dst_ref=(gath_f.at[me], craw)[k],
            send_sem=pipe_send.at[k],
            recv_sem=pipe_recv.at[k],
            device_id={"pipe": (ahead, behind)[k]},
            device_id_type=MESH,
        )

    shift(0).start()
    shift(1).start()

    gap = jnp.zeros((units, 2 * LANES - width), BF16)
    for z in range(ring):
        columns = slice(z * width, (z + 1) * width)
        wgu[z, :units, :] = jnp.concatenate([wg_ref[:, columns], gap], axis=1)
        wgu[z, units:, :] = jnp.concatenate([wu_ref[:, columns], gap], axis=1)
        wdn[z] = jnp.concatenate([wd_ref[:, columns], gap], axis=1)

    mine = broute_ref[...] == expert
    before = (
        lax.broadcasted_iota(jnp.int32, (rows, rows), 0)
        > lax.broadcasted_iota(jnp.int32, (rows, rows), 1)
    ).astype(F32).astype(BF16)
    named = jnp.broadcast_to(mine.astype(F32), (rows, capacity))
    slot = dot(before, named.astype(BF16))
    column = lax.broadcasted_iota(jnp.int32, (rows, capacity), 1).astype(F32)
    place = jnp.where(slot == column, named, 0.0).astype(BF16)
    gate_b = dot(place, sgate_ref[...])
    upper_b = dot(place, sup_ref[...])
    sig = jax.nn.sigmoid(gate_b)
    coef_g[...] = upper_b * sig * (1.0 + gate_b * (1.0 - sig))
    coef_u[...] = gate_b * sig
    hbt[...] = jnp.transpose(gate_b * sig * upper_b).astype(BF16)

    def ring_copy(buf, slot_out, slot_in, send, recv, way, k):
        return pltpu.make_async_remote_copy(
            src_ref=buf.at[slot_out],
            dst_ref=buf.at[slot_in],
            send_sem=send.at[way, k],
            recv_sem=recv.at[way, k],
            device_id={"expert": (right, left)[way]},
            device_id_type=MESH,
        )

    def gather(stream, way, k):
        buf, send, recv = ((gath_f, gs_f, gr_f), (gath_b, gs_b, gr_b))[stream]
        shard = lax.rem(me + ring - k, ring) if way == 0 else lax.rem(me + k, ring)
        return ring_copy(buf, shard, shard, send, recv, way, k)

    def arrived(stream, way, k):
        buf, send, recv = ((gath_f, gs_f, gr_f), (gath_b, gs_b, gr_b))[stream]
        shard = lax.rem(me + ring - 1 - k, ring) if way == 0 else lax.rem(me + 1 + k, ring)
        ring_copy(buf, shard, shard, send, recv, way, k).wait_recv()
        return shard

    def use_f(shard):
        main, tail = unpack(gath_f[shard], rows, rest)
        acc_f[...] += dot_t(jnp.concatenate([main, tail], axis=1), wgu[shard])

    def use_b(shard):
        main, tail = unpack(gath_b[shard], rows, rest)
        acc_b[...] += dot_t(jnp.concatenate([main, tail], axis=1), wdn[shard])

    acc_f[...] = jnp.zeros_like(acc_f)
    acc_b[...] = jnp.zeros_like(acc_b)

    shift(0).wait_recv()
    gather(0, 0, 0).start()
    gather(0, 1, 0).start()
    shift(1).wait_recv()
    bweight = bweight_ref[...].astype(F32)
    lane = lax.broadcasted_iota(jnp.int32, (quarter, LANES), 1)
    scales = [jnp.broadcast_to(bweight, (rows, LANES))]
    for k in range(3):
        scales.append(
            jnp.where(lane < rest, bweight[k * quarter : (k + 1) * quarter], bweight[3 * quarter :])
        )
    gath_b[me] = (craw[...].astype(F32) * jnp.concatenate(scales, axis=0)).astype(BF16)
    gather(1, 0, 0).start()
    gather(1, 1, 0).start()
    use_f(me)
    use_b(me)

    def gather_both(k, carry):
        for stream, use in ((0, use_f), (1, use_b)):
            one = arrived(stream, 0, k)
            gather(stream, 0, k + 1).start()
            two = arrived(stream, 1, k)

            @pl.when(k < half - 2)
            def _():
                gather(stream, 1, k + 1).start()

            use(one)
            use(two)
        return carry

    lax.fori_loop(0, half - 1, gather_both, 0)
    last_f = arrived(0, 0, half - 1)
    use_f(last_f)
    gate = acc_f[:, :units]
    upper = acc_f[:, units:]
    hid[...] = jnp.where(
        froute_ref[...] == expert, gate * jax.nn.sigmoid(gate) * upper, 0.0
    ).astype(BF16)

    def part_f(shard):
        full = dot(hid[...], wdn[shard])
        return pack(full[:, :LANES], full[:, LANES:], rest)

    def part_b(shard):
        full = dot(dgu[...], wgu[shard])
        return pack(full[:, :LANES], full[:, LANES:], rest)

    def reduce(stream, way, k):
        buf, send, recv = ((red_f, rs_f, rr_f), (red_b, rs_b, rr_b))[stream]
        return pltpu.make_async_remote_copy(
            src_ref=buf.at[way, k],
            dst_ref=buf.at[way, k + 1],
            send_sem=send.at[way, k],
            recv_sem=recv.at[way, k],
            device_id={"expert": (right, left)[way]},
            device_id_type=MESH,
        )

    def target(way, k):
        return lax.rem(me + half - k + ring, ring) if way == 0 else lax.rem(me + ring - half + 1 + k, ring)

    for way in range(2):
        red_f[way, 0] = part_f(target(way, 0)).astype(BF16)
        reduce(0, way, 0).start()

    last_b = arrived(1, 0, half - 1)
    use_b(last_b)
    d_hidden = acc_b[...]
    dgu[:, :units] = (d_hidden * coef_g[...]).astype(BF16)
    dgu[:, units:] = (d_hidden * coef_u[...]).astype(BF16)
    for way in range(2):
        red_b[way, 0] = part_b(target(way, 0)).astype(BF16)
        reduce(1, way, 0).start()

    def down_piece(g):
        pieces = []
        for z in range(4):
            main, tail = unpack(gath_b[4 * g + z], rows, rest)
            full = dot(hbt[...], jnp.concatenate([main, tail], axis=1))
            pieces.append(full[:, :width])
        start = pl.multiple_of(g * 4 * width, LANES)
        dg[:, pl.ds(start, 4 * width)] = jnp.concatenate(pieces, axis=1)

    def reduce_step(k):
        for stream, part in ((0, part_f), (1, part_b)):
            buf = (red_f, red_b)[stream]
            reduce(stream, 0, k - 1).wait_recv()
            buf[0, k] = (buf[0, k].astype(F32) + part(target(0, k))).astype(BF16)
            reduce(stream, 0, k).start()

            @pl.when(k < half - 1)
            def _():
                reduce(stream, 1, k - 1).wait_recv()
                buf[1, k] = (buf[1, k].astype(F32) + part(target(1, k))).astype(BF16)
                reduce(stream, 1, k).start()

    groups = ring // 4

    def early(k, carry):
        reduce_step(k)
        down_piece(k - 1)
        return carry

    def late(k, carry):
        reduce_step(k)
        return carry

    def give():
        return pltpu.make_async_remote_copy(
            src_ref=dg.at[pl.ds(pl.multiple_of(peer * (units // 2), 8), units // 2)],
            dst_ref=dg_in,
            send_sem=dp_send,
            recv_sem=dp_recv,
            device_id={"dp": peer},
            device_id_type=MESH,
        )

    lax.fori_loop(1, groups + 1, early, 0)
    give().start()
    lax.fori_loop(groups + 1, half, late, 0)

    for stream, part in ((0, part_f), (1, part_b)):
        buf = (red_f, red_b)[stream]
        total = part(me)
        reduce(stream, 1, half - 2).wait_recv()
        total = total + buf[1, half - 1].astype(F32)
        reduce(stream, 0, half - 1).wait_recv()
        total = total + buf[0, half].astype(F32)
        main, tail = unpack(total, rows, rest)
        summed = jnp.concatenate([main, tail[:, :rest]], axis=1).astype(BF16).astype(F32)
        own_main, own_tail = unpack((gath_f[me], craw[...])[stream], rows, rest)
        own = jnp.concatenate([own_main, own_tail], axis=1)[:, :width].astype(F32)
        if stream == 0:
            fout_ref[...] = (own + fweight_ref[...].astype(F32) * summed).astype(BF16)
        else:
            bout_ref[...] = (own + summed).astype(BF16)

    give().wait_recv()
    mine_rows = pl.ds(pl.multiple_of(replica * (units // 2), 8), units // 2)
    dgrad_ref[...] = dg[mine_rows, :] + dg_in[...]

    shift(0).wait_send()
    shift(1).wait_send()
    give().wait_send()
    for stream in range(2):
        for way, count in ((0, half), (1, half - 1)):

            def drain(k, carry):
                gather(stream, way, k).wait_send()
                reduce(stream, way, k).wait_send()
                return carry

            lax.fori_loop(0, count, drain, 0)


def solution(mesh):
    ring = mesh.shape["expert"]
    sections = mesh.shape["pipe"]
    half = ring // 2

    def body(
        fwd_sent,
        fwd_route,
        fwd_weight,
        bwd_cot,
        bwd_route,
        bwd_weight,
        saved_gate,
        saved_up,
        gate_weight,
        up_weight,
        down_weight,
    ):
        rows, width = fwd_sent.shape[1:]
        units, model = gate_weight.shape[1:]
        dense = rows + 3 * (rows // 4)
        dma = pltpu.SemaphoreType.DMA
        vmem = pl.BlockSpec(memory_space=pltpu.VMEM)
        outs = pl.pallas_call(
            functools.partial(kernel, ring, sections),
            out_shape=(
                jax.ShapeDtypeStruct((rows, width), BF16),
                jax.ShapeDtypeStruct((rows, width), BF16),
                jax.ShapeDtypeStruct((units // 2, model), F32),
            ),
            in_specs=[vmem] * 11,
            out_specs=(vmem,) * 3,
            scratch_shapes=[
                pltpu.VMEM((dense, LANES), BF16),
                pltpu.VMEM((dense, LANES), BF16),
                pltpu.VMEM((dense, LANES), BF16),
                pltpu.VMEM((ring, dense, LANES), BF16),
                pltpu.VMEM((ring, dense, LANES), BF16),
                pltpu.VMEM((2, half + 1, dense, LANES), BF16),
                pltpu.VMEM((2, half + 1, dense, LANES), BF16),
                pltpu.VMEM((ring, 2 * units, 2 * LANES), BF16),
                pltpu.VMEM((ring, units, 2 * LANES), BF16),
                pltpu.VMEM((rows, 2 * units), F32),
                pltpu.VMEM((rows, units), F32),
                pltpu.VMEM((rows, units), F32),
                pltpu.VMEM((rows, units), F32),
                pltpu.VMEM((units, rows), BF16),
                pltpu.VMEM((rows, units), BF16),
                pltpu.VMEM((rows, 2 * units), BF16),
                pltpu.VMEM((units, model), F32),
                pltpu.VMEM((units // 2, model), F32),
                dma((2,)),
                dma((2,)),
            ]
            + [dma((2, half))] * 8
            + [dma, dma],
            compiler_params=pltpu.CompilerParams(
                collective_id=0, has_side_effects=True, vmem_limit_bytes=56 * 1024 * 1024
            ),
        )(
            fwd_sent[0],
            fwd_route[0],
            fwd_weight[0],
            bwd_cot[0],
            bwd_route[0],
            bwd_weight[0],
            saved_gate[0, 0],
            saved_up[0, 0],
            gate_weight[0],
            up_weight[0],
            down_weight[0],
        )
        return tuple(out[None] for out in outs)

    in_specs = (
        P("pipe", "dp", "expert"),
        P("pipe", "dp", None),
        P("pipe", "dp", None),
        P("pipe", "dp", "expert"),
        P("pipe", "dp", None),
        P("pipe", "dp", None),
        P("pipe", "dp", None, "expert"),
        P("pipe", "dp", None, "expert"),
        P("pipe", "expert", None),
        P("pipe", "expert", None),
        P("pipe", "expert", None),
    )
    out_specs = (
        P("pipe", "dp", "expert"),
        P("pipe", "dp", "expert"),
        P("pipe", ("expert", "dp"), None),
    )
    return jax.shard_map(body, mesh=mesh, in_specs=in_specs, out_specs=out_specs, check_vma=False)
```

```python
import functools

import jax
import jax.numpy as jnp
from jax import lax
from jax.experimental import pallas as pl
from jax.experimental.pallas import tpu as pltpu
from jax.sharding import PartitionSpec as P

EXPERTS = 2
LANES = 128
GROUP = 4
MESH = pl.DeviceIdType.MESH
BY_UNITS = (((1,), (1,)), ((), ()))
F32 = jnp.float32
BF16 = jnp.bfloat16


def dot(a, b):
    return jnp.dot(a, b, preferred_element_type=F32)


def dot_t(a, b):
    return lax.dot_general(a, b, BY_UNITS, preferred_element_type=F32)


def kernel(
    ring,
    sections,
    x_ref,
    froute_ref,
    fweight_ref,
    c_ref,
    broute_ref,
    bweight_ref,
    sgate_ref,
    sup_ref,
    wg_ref,
    wu_ref,
    wd_ref,
    fout_ref,
    bout_ref,
    dgrad_ref,
    craw,
    gath_f,
    gath_b,
    red_f,
    red_b,
    wgu,
    wdn,
    wgu_t,
    wdn_t,
    acc_f,
    acc_b,
    coef_g,
    coef_u,
    hbt,
    hid,
    dgu,
    dg,
    dg_in,
    pipe_send,
    pipe_recv,
    gs_f,
    gr_f,
    gs_b,
    gr_b,
    rs_f,
    rr_f,
    rs_b,
    rr_b,
    dp_send,
    dp_recv,
):
    width, rows = x_ref.shape
    units = wg_ref.shape[0]
    capacity = sgate_ref.shape[1]
    half = ring // 2
    groups = ring // GROUP
    me = lax.axis_index("expert")
    section = lax.axis_index("pipe")
    replica = lax.axis_index("dp")
    right, left = lax.rem(me + 1, ring), lax.rem(me + ring - 1, ring)
    ahead, behind = lax.rem(section + 1, sections), lax.rem(section + sections - 1, sections)
    peer = 1 - replica
    expert = me // (ring // EXPERTS)

    barrier = pltpu.get_barrier_semaphore()
    for axis, other in (
        ("expert", right),
        ("expert", left),
        ("pipe", ahead),
        ("pipe", behind),
        ("dp", peer),
    ):
        pl.semaphore_signal(barrier, inc=1, device_id={axis: other}, device_id_type=MESH)
    pl.semaphore_wait(barrier, 5)

    def shift(k):
        return pltpu.make_async_remote_copy(
            src_ref=(x_ref, c_ref)[k],
            dst_ref=(gath_f.at[me], craw)[k],
            send_sem=pipe_send.at[k],
            recv_sem=pipe_recv.at[k],
            device_id={"pipe": (ahead, behind)[k]},
            device_id_type=MESH,
        )

    shift(0).start()
    shift(1).start()

    def split_weights(g, carry):
        columns = pl.ds(pl.multiple_of(g * (GROUP * width), LANES), GROUP * width)
        both = jnp.concatenate([wg_ref[:, columns], wu_ref[:, columns]], axis=0)
        down = wd_ref[:, columns]
        for z in range(GROUP):
            piece = both[:, z * width : (z + 1) * width]
            wgu[GROUP * g + z] = piece
            wgu_t[GROUP * g + z] = jnp.transpose(piece)
            piece = down[:, z * width : (z + 1) * width]
            wdn[GROUP * g + z] = piece
            wdn_t[GROUP * g + z] = jnp.transpose(piece)
        return carry

    def gather_copy(stream, way, k, shard):
        buf, send, recv = ((gath_f, gs_f, gr_f), (gath_b, gs_b, gr_b))[stream]
        return pltpu.make_async_remote_copy(
            src_ref=buf.at[shard],
            dst_ref=buf.at[shard],
            send_sem=send.at[way, k],
            recv_sem=recv.at[way, k],
            device_id={"expert": (right, left)[way]},
            device_id_type=MESH,
        )

    def gather(stream, way, k):
        shard = lax.rem(me + ring - k, ring) if way == 0 else lax.rem(me + k, ring)
        return gather_copy(stream, way, k, shard)

    def arrived(stream, way, k):
        shard = lax.rem(me + ring - 1 - k, ring) if way == 0 else lax.rem(me + 1 + k, ring)
        gather_copy(stream, way, k, shard).wait_recv()
        return shard

    def use_f(shard):
        acc_f[...] += dot(wgu[shard], gath_f[shard])

    def use_b(shard):
        acc_b[...] += dot(wdn[shard], gath_b[shard])

    acc_f[...] = jnp.zeros_like(acc_f)
    acc_b[...] = jnp.zeros_like(acc_b)

    shift(0).wait_recv()
    gather(0, 0, 0).start()
    gather(0, 1, 0).start()
    shift(1).wait_recv()
    gath_b[me] = (craw[...].astype(F32) * bweight_ref[...].astype(F32)).astype(BF16)
    gather(1, 0, 0).start()
    gather(1, 1, 0).start()

    lax.fori_loop(0, groups, split_weights, 0)

    before = (
        lax.broadcasted_iota(jnp.int32, (rows, rows), 0)
        < lax.broadcasted_iota(jnp.int32, (rows, rows), 1)
    ).astype(F32).astype(BF16)
    named = jnp.broadcast_to((broute_ref[...] == expert).astype(F32), (capacity, rows))
    slot = dot(named.astype(BF16), before)
    column = lax.broadcasted_iota(jnp.int32, (capacity, rows), 0).astype(F32)
    place = jnp.where(slot == column, named, 0.0).astype(BF16)
    gate_b = dot(sgate_ref[...], place)
    upper_b = dot(sup_ref[...], place)
    sig = jax.nn.sigmoid(gate_b)
    coef_g[...] = upper_b * sig * (1.0 + gate_b * (1.0 - sig))
    coef_u[...] = gate_b * sig
    hbt[...] = (gate_b * sig * upper_b).astype(BF16)

    use_f(me)
    use_b(me)

    def gather_both(k, carry):
        for stream, use in ((0, use_f), (1, use_b)):
            one = arrived(stream, 0, k)
            gather(stream, 0, k + 1).start()
            two = arrived(stream, 1, k)

            @pl.when(k < half - 2)
            def _():
                gather(stream, 1, k + 1).start()

            use(one)
            use(two)
        return carry

    lax.fori_loop(0, half - 1, gather_both, 0)
    use_f(arrived(0, 0, half - 1))
    gate = acc_f[:units]
    upper = acc_f[units:]
    hid[...] = jnp.where(
        froute_ref[...] == expert, gate * jax.nn.sigmoid(gate) * upper, 0.0
    ).astype(BF16)

    def part_f(shard):
        return dot(wdn_t[shard], hid[...])

    def part_b(shard):
        return dot(wgu_t[shard], dgu[...])

    def reduce(stream, way, k):
        buf, send, recv = ((red_f, rs_f, rr_f), (red_b, rs_b, rr_b))[stream]
        return pltpu.make_async_remote_copy(
            src_ref=buf.at[way, k],
            dst_ref=buf.at[way, k + 1],
            send_sem=send.at[way, k],
            recv_sem=recv.at[way, k],
            device_id={"expert": (right, left)[way]},
            device_id_type=MESH,
        )

    def target(way, k):
        return lax.rem(me + half - k + ring, ring) if way == 0 else lax.rem(me + ring - half + 1 + k, ring)

    for way in range(2):
        red_f[way, 0] = part_f(target(way, 0)).astype(BF16)
        reduce(0, way, 0).start()

    use_b(arrived(1, 0, half - 1))
    d_hidden = acc_b[...]
    dgu[:units] = (d_hidden * coef_g[...]).astype(BF16)
    dgu[units:] = (d_hidden * coef_u[...]).astype(BF16)
    for way in range(2):
        red_b[way, 0] = part_b(target(way, 0)).astype(BF16)
        reduce(1, way, 0).start()

    def down_piece(g):
        shards = gath_b[pl.ds(GROUP * g, GROUP)].reshape(GROUP * width, rows)
        start = pl.multiple_of(g * (GROUP * width), LANES)
        dg[:, pl.ds(start, GROUP * width)] = dot_t(hbt[...], shards)

    def reduce_step(k):
        for stream, part in ((0, part_f), (1, part_b)):
            buf = (red_f, red_b)[stream]
            term = part(target(0, k))
            reduce(stream, 0, k - 1).wait_recv()
            buf[0, k] = (buf[0, k].astype(F32) + term).astype(BF16)
            reduce(stream, 0, k).start()

            @pl.when(k < half - 1)
            def _():
                term = part(target(1, k))
                reduce(stream, 1, k - 1).wait_recv()
                buf[1, k] = (buf[1, k].astype(F32) + term).astype(BF16)
                reduce(stream, 1, k).start()

    def early(k, carry):
        reduce_step(k)
        down_piece(k - 1)
        return carry

    def late(k, carry):
        reduce_step(k)
        return carry

    def give():
        return pltpu.make_async_remote_copy(
            src_ref=dg.at[pl.ds(pl.multiple_of(peer * (units // 2), 8), units // 2)],
            dst_ref=dg_in,
            send_sem=dp_send,
            recv_sem=dp_recv,
            device_id={"dp": peer},
            device_id_type=MESH,
        )

    lax.fori_loop(1, groups + 1, early, 0)
    give().start()
    lax.fori_loop(groups + 1, half, late, 0)

    give().wait_recv()
    mine_rows = pl.ds(pl.multiple_of(replica * (units // 2), 8), units // 2)
    dgrad_ref[...] = dg[mine_rows, :] + dg_in[...]

    for stream, part in ((0, part_f), (1, part_b)):
        buf = (red_f, red_b)[stream]
        total = part(me)
        reduce(stream, 1, half - 2).wait_recv()
        total = total + buf[1, half - 1].astype(F32)
        reduce(stream, 0, half - 1).wait_recv()
        total = total + buf[0, half].astype(F32)
        summed = total.astype(BF16).astype(F32)
        if stream == 0:
            fout_ref[...] = (
                gath_f[me].astype(F32) + fweight_ref[...].astype(F32) * summed
            ).astype(BF16)
        else:
            bout_ref[...] = (craw[...].astype(F32) + summed).astype(BF16)

    shift(0).wait_send()
    shift(1).wait_send()
    give().wait_send()
    for stream in range(2):
        for way, count in ((0, half), (1, half - 1)):

            def drain(k, carry):
                gather(stream, way, k).wait_send()
                reduce(stream, way, k).wait_send()
                return carry

            lax.fori_loop(0, count, drain, 0)


def solution(mesh):
    ring = mesh.shape["expert"]
    sections = mesh.shape["pipe"]
    half = ring // 2

    def body(
        fwd_sent,
        fwd_route,
        fwd_weight,
        bwd_cot,
        bwd_route,
        bwd_weight,
        saved_gate,
        saved_up,
        gate_weight,
        up_weight,
        down_weight,
    ):
        rows, width = fwd_sent.shape[1:]
        units, model = gate_weight.shape[1:]
        dma = pltpu.SemaphoreType.DMA
        vmem = pl.BlockSpec(memory_space=pltpu.VMEM)
        outs = pl.pallas_call(
            functools.partial(kernel, ring, sections),
            out_shape=(
                jax.ShapeDtypeStruct((width, rows), BF16),
                jax.ShapeDtypeStruct((width, rows), BF16),
                jax.ShapeDtypeStruct((units // 2, model), F32),
            ),
            in_specs=[vmem] * 11,
            out_specs=(vmem,) * 3,
            scratch_shapes=[
                pltpu.VMEM((width, rows), BF16),
                pltpu.VMEM((ring, width, rows), BF16),
                pltpu.VMEM((ring, width, rows), BF16),
                pltpu.VMEM((2, half + 1, width, rows), BF16),
                pltpu.VMEM((2, half + 1, width, rows), BF16),
                pltpu.VMEM((ring, 2 * units, width), BF16),
                pltpu.VMEM((ring, units, width), BF16),
                pltpu.VMEM((ring, width, 2 * units), BF16),
                pltpu.VMEM((ring, width, units), BF16),
                pltpu.VMEM((2 * units, rows), F32),
                pltpu.VMEM((units, rows), F32),
                pltpu.VMEM((units, rows), F32),
                pltpu.VMEM((units, rows), F32),
                pltpu.VMEM((units, rows), BF16),
                pltpu.VMEM((units, rows), BF16),
                pltpu.VMEM((2 * units, rows), BF16),
                pltpu.VMEM((units, model), F32),
                pltpu.VMEM((units // 2, model), F32),
                dma((2,)),
                dma((2,)),
            ]
            + [dma((2, half))] * 8
            + [dma, dma],
            compiler_params=pltpu.CompilerParams(
                collective_id=0, has_side_effects=True, vmem_limit_bytes=56 * 1024 * 1024
            ),
        )(
            fwd_sent[0].T,
            fwd_route[0].T,
            fwd_weight[0].T,
            bwd_cot[0].T,
            bwd_route[0].T,
            bwd_weight[0].T,
            saved_gate[0, 0].T,
            saved_up[0, 0].T,
            gate_weight[0],
            up_weight[0],
            down_weight[0],
        )
        return outs[0].T[None], outs[1].T[None], outs[2][None]

    in_specs = (
        P("pipe", "dp", "expert"),
        P("pipe", "dp", None),
        P("pipe", "dp", None),
        P("pipe", "dp", "expert"),
        P("pipe", "dp", None),
        P("pipe", "dp", None),
        P("pipe", "dp", None, "expert"),
        P("pipe", "dp", None, "expert"),
        P("pipe", "expert", None),
        P("pipe", "expert", None),
        P("pipe", "expert", None),
    )
    out_specs = (
        P("pipe", "dp", "expert"),
        P("pipe", "dp", "expert"),
        P("pipe", ("expert", "dp"), None),
    )
    return jax.shard_map(body, mesh=mesh, in_specs=in_specs, out_specs=out_specs, check_vma=False)
```

```python
import functools

import jax
import jax.numpy as jnp
from jax import lax
from jax.experimental import pallas as pl
from jax.experimental.pallas import tpu as pltpu
from jax.sharding import PartitionSpec as P

EXPERTS = 2
LANES = 128
GROUP = 4
MESH = pl.DeviceIdType.MESH
BY_UNITS = (((1,), (1,)), ((), ()))
F32 = jnp.float32
BF16 = jnp.bfloat16


def dot(a, b):
    return jnp.dot(a, b, preferred_element_type=F32)


def dot_t(a, b):
    return lax.dot_general(a, b, BY_UNITS, preferred_element_type=F32)


def kernel(
    ring,
    sections,
    x_ref,
    froute_ref,
    fweight_ref,
    c_ref,
    broute_ref,
    bweight_ref,
    sgate_ref,
    sup_ref,
    wg_ref,
    wu_ref,
    wd_ref,
    fout_ref,
    bout_ref,
    dgrad_ref,
    gath_f,
    gath_b,
    red_f,
    red_b,
    wgu,
    wdn,
    wgu_t,
    wdn_t,
    acc_f,
    acc_b,
    coef_g,
    coef_u,
    hbt,
    hid,
    dgu,
    dg,
    dg_in,
    pipe_send,
    pipe_recv,
    gs,
    gr,
    rs,
    rr,
    dp_send,
    dp_recv,
):
    width, rows = x_ref.shape
    units = wg_ref.shape[0]
    capacity = sgate_ref.shape[1]
    half = ring // 2
    groups = ring // GROUP
    me = lax.axis_index("expert")
    section = lax.axis_index("pipe")
    replica = lax.axis_index("dp")
    right, left = lax.rem(me + 1, ring), lax.rem(me + ring - 1, ring)
    ahead, behind = lax.rem(section + 1, sections), lax.rem(section + sections - 1, sections)
    peer = 1 - replica
    expert = me // (ring // EXPERTS)

    part_width = width // 2
    hops = ((half, half - 1), (half - 1, half))
    flows = [(stream, h) for h in range(2) for stream in range(2)]
    sides = (right, left)
    stage = (ahead, behind)

    barrier = pltpu.get_barrier_semaphore()
    partners = [{"expert": right}, {"expert": left}, {"dp": peer}]
    for section_to in stage:
        partners.append({"pipe": section_to})
        partners += [{"pipe": section_to, "expert": side} for side in sides]
    for partner in partners:
        pl.semaphore_signal(barrier, inc=1, device_id=partner, device_id_type=MESH)
    pl.semaphore_wait(barrier, len(partners))

    def band(h):
        return pl.ds(h * part_width, part_width)

    def shift(stream):
        return pltpu.make_async_remote_copy(
            src_ref=(x_ref, c_ref)[stream],
            dst_ref=(gath_f, gath_b)[stream].at[me],
            send_sem=pipe_send.at[stream],
            recv_sem=pipe_recv.at[stream],
            device_id={"pipe": stage[stream]},
            device_id_type=MESH,
        )

    def first(stream, h, way):
        return pltpu.make_async_remote_copy(
            src_ref=(x_ref, c_ref)[stream].at[band(h)],
            dst_ref=(gath_f, gath_b)[stream].at[me, band(h)],
            send_sem=gs.at[stream, h, way, 0],
            recv_sem=gr.at[stream, h, way, 0],
            device_id={"pipe": stage[stream], "expert": sides[way]},
            device_id_type=MESH,
        )

    for stream, h in flows:
        for way in range(2):
            first(stream, h, way).start()
    for stream in range(2):
        shift(stream).start()

    def split_weights(g, carry):
        columns = pl.ds(pl.multiple_of(g * (GROUP * width), LANES), GROUP * width)
        both = jnp.concatenate([wg_ref[:, columns], wu_ref[:, columns]], axis=0)
        down = wd_ref[:, columns]
        for z in range(GROUP):
            piece = both[:, z * width : (z + 1) * width]
            wgu[GROUP * g + z] = piece
            wgu_t[GROUP * g + z] = jnp.transpose(piece)
            piece = down[:, z * width : (z + 1) * width]
            wdn[GROUP * g + z] = piece
            wdn_t[GROUP * g + z] = jnp.transpose(piece)
        return carry

    def gather_copy(stream, h, way, k, shard):
        piece = (gath_f, gath_b)[stream].at[shard, band(h)]
        return pltpu.make_async_remote_copy(
            src_ref=piece,
            dst_ref=piece,
            send_sem=gs.at[stream, h, way, k],
            recv_sem=gr.at[stream, h, way, k],
            device_id={"expert": sides[way]},
            device_id_type=MESH,
        )

    def source(way, k):
        return lax.rem(me + ring - 1 - k, ring) if way == 0 else lax.rem(me + 1 + k, ring)

    def arrived(stream, h, way, k):
        gather_copy(stream, h, way, k, source(way, k)).wait_recv()

    def forward(stream, h, way, k):
        return gather_copy(stream, h, way, k + 1, source(way, k))

    bweight = bweight_ref[...].astype(F32)

    def use_f(shard):
        acc_f[...] += dot(wgu[shard], gath_f[shard])

    def use_b(shard):
        cot = (gath_b[shard].astype(F32) * bweight).astype(BF16)
        acc_b[...] += dot(wdn[shard], cot)

    acc_f[...] = jnp.zeros_like(acc_f)
    acc_b[...] = jnp.zeros_like(acc_b)

    lax.fori_loop(0, groups, split_weights, 0)

    before = (
        lax.broadcasted_iota(jnp.int32, (rows, rows), 0)
        < lax.broadcasted_iota(jnp.int32, (rows, rows), 1)
    ).astype(F32).astype(BF16)
    named = jnp.broadcast_to((broute_ref[...] == expert).astype(F32), (capacity, rows))
    slot = dot(named.astype(BF16), before)
    column = lax.broadcasted_iota(jnp.int32, (capacity, rows), 0).astype(F32)
    place = jnp.where(slot == column, named, 0.0).astype(BF16)
    gate_b = dot(sgate_ref[...], place)
    upper_b = dot(sup_ref[...], place)
    sig = jax.nn.sigmoid(gate_b)
    coef_g[...] = upper_b * sig * (1.0 + gate_b * (1.0 - sig))
    coef_u[...] = gate_b * sig
    hbt[...] = (gate_b * sig * upper_b).astype(BF16)

    shift(0).wait_recv()
    use_f(me)
    shift(1).wait_recv()
    use_b(me)

    def gather_all(k, carry):
        for stream, h in flows:
            for way in range(2):
                arrived(stream, h, way, k)
                if hops[h][way] == half:
                    forward(stream, h, way, k).start()
                else:

                    @pl.when(k < half - 2)
                    def _():
                        forward(stream, h, way, k).start()

            if h == 1:
                for way in range(2):
                    (use_f, use_b)[stream](source(way, k))
        return carry

    lax.fori_loop(0, half - 1, gather_all, 0)
    for h in range(2):
        arrived(0, h, h, half - 1)
    use_f(source(0, half - 1))
    gate = acc_f[:units]
    upper = acc_f[units:]
    hid[...] = jnp.where(
        froute_ref[...] == expert, gate * jax.nn.sigmoid(gate) * upper, 0.0
    ).astype(BF16)

    def part(stream, h, shard):
        if stream == 0:
            return dot(wdn_t[shard, band(h)], hid[...])
        return dot(wgu_t[shard, band(h)], dgu[...])

    def reduce(stream, h, way, k):
        buf = (red_f, red_b)[stream]
        return pltpu.make_async_remote_copy(
            src_ref=buf.at[h, way, k],
            dst_ref=buf.at[h, way, k + 1],
            send_sem=rs.at[stream, h, way, k],
            recv_sem=rr.at[stream, h, way, k],
            device_id={"expert": sides[way]},
            device_id_type=MESH,
        )

    def target(h, way, k):
        ahead_by = hops[h][way] - k
        return lax.rem(me + (ahead_by if way == 0 else ring - ahead_by), ring)

    def begin(stream):
        for h in range(2):
            for way in range(2):
                (red_f, red_b)[stream][h, way, 0] = part(stream, h, target(h, way, 0)).astype(BF16)
                reduce(stream, h, way, 0).start()

    begin(0)
    for h in range(2):
        arrived(1, h, h, half - 1)
    use_b(source(0, half - 1))
    d_hidden = acc_b[...]
    dgu[:units] = (d_hidden * coef_g[...]).astype(BF16)
    dgu[units:] = (d_hidden * coef_u[...]).astype(BF16)
    begin(1)

    def down_piece(g):
        raw = gath_b[pl.ds(GROUP * g, GROUP)].reshape(GROUP * width, rows)
        shards = (raw.astype(F32) * bweight).astype(BF16)
        start = pl.multiple_of(g * (GROUP * width), LANES)
        dg[:, pl.ds(start, GROUP * width)] = dot_t(hbt[...], shards)

    def relay(stream, h, way, k):
        buf = (red_f, red_b)[stream]
        term = part(stream, h, target(h, way, k))
        reduce(stream, h, way, k - 1).wait_recv()
        buf[h, way, k] = (buf[h, way, k].astype(F32) + term).astype(BF16)
        reduce(stream, h, way, k).start()

    def reduce_step(k):
        for stream, h in flows:
            for way in range(2):
                if hops[h][way] == half:
                    relay(stream, h, way, k)
                else:

                    @pl.when(k < half - 1)
                    def _():
                        relay(stream, h, way, k)

    def early(k, carry):
        reduce_step(k)
        down_piece(k - 1)
        return carry

    def late(k, carry):
        reduce_step(k)
        return carry

    def give():
        return pltpu.make_async_remote_copy(
            src_ref=dg.at[pl.ds(pl.multiple_of(peer * (units // 2), 8), units // 2)],
            dst_ref=dg_in,
            send_sem=dp_send,
            recv_sem=dp_recv,
            device_id={"dp": peer},
            device_id_type=MESH,
        )

    lax.fori_loop(1, groups + 1, early, 0)
    give().start()
    lax.fori_loop(groups + 1, half, late, 0)

    give().wait_recv()
    mine_rows = pl.ds(pl.multiple_of(replica * (units // 2), 8), units // 2)
    dgrad_ref[...] = dg[mine_rows, :] + dg_in[...]

    for stream, h in flows:
        buf = (red_f, red_b)[stream]
        total = part(stream, h, me)
        for way in (1 - h, h):
            last = hops[h][way]
            reduce(stream, h, way, last - 1).wait_recv()
            total = total + buf[h, way, last].astype(F32)
        summed = total.astype(BF16).astype(F32)
        if stream == 0:
            own = gath_f[me, band(h)].astype(F32)
            fout_ref[band(h)] = (own + fweight_ref[...].astype(F32) * summed).astype(BF16)
        else:
            bout_ref[band(h)] = (gath_b[me, band(h)].astype(F32) + summed).astype(BF16)

    shift(0).wait_send()
    shift(1).wait_send()
    give().wait_send()
    for stream, h in flows:
        for way in range(2):
            first(stream, h, way).wait_send()
            reduce(stream, h, way, 0).wait_send()

            def drain(k, carry):
                gather_copy(stream, h, way, k, me).wait_send()
                reduce(stream, h, way, k).wait_send()
                return carry

            lax.fori_loop(1, hops[h][way], drain, 0)


def solution(mesh):
    ring = mesh.shape["expert"]
    sections = mesh.shape["pipe"]
    half = ring // 2

    def body(
        fwd_sent,
        fwd_route,
        fwd_weight,
        bwd_cot,
        bwd_route,
        bwd_weight,
        saved_gate,
        saved_up,
        gate_weight,
        up_weight,
        down_weight,
    ):
        rows, width = fwd_sent.shape[1:]
        units, model = gate_weight.shape[1:]
        dma = pltpu.SemaphoreType.DMA
        vmem = pl.BlockSpec(memory_space=pltpu.VMEM)
        outs = pl.pallas_call(
            functools.partial(kernel, ring, sections),
            out_shape=(
                jax.ShapeDtypeStruct((width, rows), BF16),
                jax.ShapeDtypeStruct((width, rows), BF16),
                jax.ShapeDtypeStruct((units // 2, model), F32),
            ),
            in_specs=[vmem] * 11,
            out_specs=(vmem,) * 3,
            scratch_shapes=[
                pltpu.VMEM((ring, width, rows), BF16),
                pltpu.VMEM((ring, width, rows), BF16),
                pltpu.VMEM((2, 2, half + 1, width // 2, rows), BF16),
                pltpu.VMEM((2, 2, half + 1, width // 2, rows), BF16),
                pltpu.VMEM((ring, 2 * units, width), BF16),
                pltpu.VMEM((ring, units, width), BF16),
                pltpu.VMEM((ring, width, 2 * units), BF16),
                pltpu.VMEM((ring, width, units), BF16),
                pltpu.VMEM((2 * units, rows), F32),
                pltpu.VMEM((units, rows), F32),
                pltpu.VMEM((units, rows), F32),
                pltpu.VMEM((units, rows), F32),
                pltpu.VMEM((units, rows), BF16),
                pltpu.VMEM((units, rows), BF16),
                pltpu.VMEM((2 * units, rows), BF16),
                pltpu.VMEM((units, model), F32),
                pltpu.VMEM((units // 2, model), F32),
                dma((2,)),
                dma((2,)),
            ]
            + [dma((2, 2, 2, half))] * 4
            + [dma, dma],
            compiler_params=pltpu.CompilerParams(
                collective_id=0, has_side_effects=True, vmem_limit_bytes=56 * 1024 * 1024
            ),
        )(
            fwd_sent[0].T,
            fwd_route[0].T,
            fwd_weight[0].T,
            bwd_cot[0].T,
            bwd_route[0].T,
            bwd_weight[0].T,
            saved_gate[0, 0].T,
            saved_up[0, 0].T,
            gate_weight[0],
            up_weight[0],
            down_weight[0],
        )
        return outs[0].T[None], outs[1].T[None], outs[2][None]

    in_specs = (
        P("pipe", "dp", "expert"),
        P("pipe", "dp", None),
        P("pipe", "dp", None),
        P("pipe", "dp", "expert"),
        P("pipe", "dp", None),
        P("pipe", "dp", None),
        P("pipe", "dp", None, "expert"),
        P("pipe", "dp", None, "expert"),
        P("pipe", "expert", None),
        P("pipe", "expert", None),
        P("pipe", "expert", None),
    )
    out_specs = (
        P("pipe", "dp", "expert"),
        P("pipe", "dp", "expert"),
        P("pipe", ("expert", "dp"), None),
    )
    return jax.shard_map(body, mesh=mesh, in_specs=in_specs, out_specs=out_specs, check_vma=False)
```

```python
import functools

import jax
import jax.numpy as jnp
from jax import lax
from jax.experimental import pallas as pl
from jax.experimental.pallas import tpu as pltpu
from jax.sharding import PartitionSpec as P

EXPERTS = 2
LANES = 128
GROUP = 4
MESH = pl.DeviceIdType.MESH
BY_UNITS = (((1,), (1,)), ((), ()))
F32 = jnp.float32
BF16 = jnp.bfloat16


def dot(a, b):
    return jnp.dot(a, b, preferred_element_type=F32)


def dot_t(a, b):
    return lax.dot_general(a, b, BY_UNITS, preferred_element_type=F32)


def kernel(
    ring,
    sections,
    x_ref,
    froute_ref,
    fweight_ref,
    c_ref,
    broute_ref,
    bweight_ref,
    sgate_ref,
    sup_ref,
    wg_hbm,
    wu_hbm,
    wd_hbm,
    fout_ref,
    bout_ref,
    own_ref,
    peer_ref,
    wg_ref,
    wu_ref,
    wd_ref,
    gath_f,
    gath_b,
    red_f,
    red_b,
    wgu,
    wdn,
    wgu_t,
    wdn_t,
    acc_f,
    acc_b,
    coef_g,
    coef_u,
    hbt,
    hid,
    dgu,
    dg,
    load_sem,
    keep_sem,
    pipe_send,
    pipe_recv,
    gs,
    gr,
    rs,
    rr,
    dp_send,
    dp_recv,
):
    width, rows = x_ref.shape
    units = wg_ref.shape[0]
    capacity = sgate_ref.shape[1]
    half = ring // 2
    groups = ring // GROUP
    me = lax.axis_index("expert")
    section = lax.axis_index("pipe")
    replica = lax.axis_index("dp")
    right, left = lax.rem(me + 1, ring), lax.rem(me + ring - 1, ring)
    ahead, behind = lax.rem(section + 1, sections), lax.rem(section + sections - 1, sections)
    peer = 1 - replica
    expert = me // (ring // EXPERTS)

    part_width = width // 2
    hops = ((half, half - 1), (half - 1, half))
    flows = [(stream, h) for h in range(2) for stream in range(2)]
    sides = (right, left)
    stage = (ahead, behind)

    loads = [
        pltpu.make_async_copy(hbm, ref, load_sem.at[i])
        for i, (hbm, ref) in enumerate(((wg_hbm, wg_ref), (wu_hbm, wu_ref), (wd_hbm, wd_ref)))
    ]
    for load in loads:
        load.start()

    barrier = pltpu.get_barrier_semaphore()
    partners = [{"expert": right}, {"expert": left}, {"dp": peer}]
    for section_to in stage:
        partners.append({"pipe": section_to})
        partners += [{"pipe": section_to, "expert": side} for side in sides]
    for partner in partners:
        pl.semaphore_signal(barrier, inc=1, device_id=partner, device_id_type=MESH)
    pl.semaphore_wait(barrier, len(partners))

    def band(h):
        return pl.ds(h * part_width, part_width)

    def shift(stream):
        return pltpu.make_async_remote_copy(
            src_ref=(x_ref, c_ref)[stream],
            dst_ref=(gath_f, gath_b)[stream].at[me],
            send_sem=pipe_send.at[stream],
            recv_sem=pipe_recv.at[stream],
            device_id={"pipe": stage[stream]},
            device_id_type=MESH,
        )

    def first(stream, h, way):
        return pltpu.make_async_remote_copy(
            src_ref=(x_ref, c_ref)[stream].at[band(h)],
            dst_ref=(gath_f, gath_b)[stream].at[me, band(h)],
            send_sem=gs.at[stream, h, way, 0],
            recv_sem=gr.at[stream, h, way, 0],
            device_id={"pipe": stage[stream], "expert": sides[way]},
            device_id_type=MESH,
        )

    for stream, h in flows:
        for way in range(2):
            first(stream, h, way).start()
    for stream in range(2):
        shift(stream).start()

    def split_weights(g):
        columns = pl.ds(pl.multiple_of(g * (GROUP * width), LANES), GROUP * width)
        both = jnp.concatenate([wg_ref[:, columns], wu_ref[:, columns]], axis=0)
        down = wd_ref[:, columns]
        for z in range(GROUP):
            piece = both[:, z * width : (z + 1) * width]
            wgu[GROUP * g + z] = piece
            wgu_t[GROUP * g + z] = jnp.transpose(piece)
            piece = down[:, z * width : (z + 1) * width]
            wdn[GROUP * g + z] = piece
            wdn_t[GROUP * g + z] = jnp.transpose(piece)

    def gather_copy(stream, h, way, k, shard):
        piece = (gath_f, gath_b)[stream].at[shard, band(h)]
        return pltpu.make_async_remote_copy(
            src_ref=piece,
            dst_ref=piece,
            send_sem=gs.at[stream, h, way, k],
            recv_sem=gr.at[stream, h, way, k],
            device_id={"expert": sides[way]},
            device_id_type=MESH,
        )

    def source(way, k):
        return lax.rem(me + ring - 1 - k, ring) if way == 0 else lax.rem(me + 1 + k, ring)

    def arrived(stream, h, way, k):
        gather_copy(stream, h, way, k, source(way, k)).wait_recv()

    def forward(stream, h, way, k):
        return gather_copy(stream, h, way, k + 1, source(way, k))

    bweight = bweight_ref[...].astype(F32)

    def use_f(shard):
        acc_f[...] += dot(wgu[shard], gath_f[shard])

    def use_b(shard):
        cot = (gath_b[shard].astype(F32) * bweight).astype(BF16)
        acc_b[...] += dot(wdn[shard], cot)

    acc_f[...] = jnp.zeros_like(acc_f)
    acc_b[...] = jnp.zeros_like(acc_b)

    before = (
        lax.broadcasted_iota(jnp.int32, (rows, rows), 0)
        < lax.broadcasted_iota(jnp.int32, (rows, rows), 1)
    ).astype(F32).astype(BF16)
    named = jnp.broadcast_to((broute_ref[...] == expert).astype(F32), (capacity, rows))
    slot = dot(named.astype(BF16), before)
    column = lax.broadcasted_iota(jnp.int32, (capacity, rows), 0).astype(F32)
    place = jnp.where(slot == column, named, 0.0).astype(BF16)
    gate_b = dot(sgate_ref[...], place)
    upper_b = dot(sup_ref[...], place)
    sig = jax.nn.sigmoid(gate_b)
    coef_g[...] = upper_b * sig * (1.0 + gate_b * (1.0 - sig))
    coef_u[...] = gate_b * sig
    hbt[...] = (gate_b * sig * upper_b).astype(BF16)

    def pass_on(stream, h, k):
        for way in range(2):
            arrived(stream, h, way, k)
            if hops[h][way] == half:
                forward(stream, h, way, k).start()
            else:

                @pl.when(k < half - 2)
                def _():
                    forward(stream, h, way, k).start()

    def use(k):
        for way in range(2):
            use_f(source(way, k))
            use_b(source(way, k))

    both = 2 - groups % 2
    opening = groups // both

    def gather_first(k, carry):
        for stream, h in flows:
            pass_on(stream, h, k)
            if stream == 1 and h < both:
                split_weights(both * k + h)
        return carry

    def gather_rest(k, carry):
        for stream, h in flows:
            pass_on(stream, h, k)

        @pl.when(k < 2 * opening)
        def _():
            use(k - opening)

        use(k)
        return carry

    for load in loads:
        load.wait()
    lax.fori_loop(0, opening, gather_first, 0)
    shift(0).wait_recv()
    use_f(me)
    shift(1).wait_recv()
    use_b(me)
    lax.fori_loop(opening, half - 1, gather_rest, 0)
    for k in range(half - 1 - opening, opening):
        use(k)
    for h in range(2):
        arrived(0, h, h, half - 1)
    use_f(source(0, half - 1))
    gate = acc_f[:units]
    upper = acc_f[units:]
    hid[...] = jnp.where(
        froute_ref[...] == expert, gate * jax.nn.sigmoid(gate) * upper, 0.0
    ).astype(BF16)

    def part(stream, h, shard):
        if stream == 0:
            return dot(wdn_t[shard, band(h)], hid[...])
        return dot(wgu_t[shard, band(h)], dgu[...])

    def reduce(stream, h, way, k):
        buf = (red_f, red_b)[stream]
        return pltpu.make_async_remote_copy(
            src_ref=buf.at[h, way, k],
            dst_ref=buf.at[h, way, k + 1],
            send_sem=rs.at[stream, h, way, k],
            recv_sem=rr.at[stream, h, way, k],
            device_id={"expert": sides[way]},
            device_id_type=MESH,
        )

    def target(h, way, k):
        ahead_by = hops[h][way] - k
        return lax.rem(me + (ahead_by if way == 0 else ring - ahead_by), ring)

    def begin(stream):
        for h in range(2):
            for way in range(2):
                (red_f, red_b)[stream][h, way, 0] = part(stream, h, target(h, way, 0)).astype(BF16)
                reduce(stream, h, way, 0).start()

    begin(0)
    for h in range(2):
        arrived(1, h, h, half - 1)
    use_b(source(0, half - 1))
    d_hidden = acc_b[...]
    dgu[:units] = (d_hidden * coef_g[...]).astype(BF16)
    dgu[units:] = (d_hidden * coef_u[...]).astype(BF16)
    begin(1)

    def down_piece(g):
        raw = gath_b[pl.ds(GROUP * g, GROUP)].reshape(GROUP * width, rows)
        shards = (raw.astype(F32) * bweight).astype(BF16)
        start = pl.multiple_of(g * (GROUP * width), LANES)
        dg[:, pl.ds(start, GROUP * width)] = dot_t(hbt[...], shards)

    def relay(stream, h, way, k):
        buf = (red_f, red_b)[stream]
        term = part(stream, h, target(h, way, k))
        reduce(stream, h, way, k - 1).wait_recv()
        buf[h, way, k] = (buf[h, way, k].astype(F32) + term).astype(BF16)
        reduce(stream, h, way, k).start()

    def reduce_step(k):
        for stream, h in flows:
            for way in range(2):
                if hops[h][way] == half:
                    relay(stream, h, way, k)
                else:

                    @pl.when(k < half - 1)
                    def _():
                        relay(stream, h, way, k)

    def early(k, carry):
        reduce_step(k)
        down_piece(k - 1)
        return carry

    def late(k, carry):
        reduce_step(k)
        return carry

    def give():
        return pltpu.make_async_remote_copy(
            src_ref=dg.at[pl.ds(pl.multiple_of(peer * (units // 2), 8), units // 2)],
            dst_ref=peer_ref,
            send_sem=dp_send,
            recv_sem=dp_recv,
            device_id={"dp": peer},
            device_id_type=MESH,
        )

    mine_rows = pl.ds(pl.multiple_of(replica * (units // 2), 8), units // 2)
    keep = pltpu.make_async_copy(dg.at[mine_rows], own_ref, keep_sem)

    lax.fori_loop(1, groups + 1, early, 0)
    give().start()
    keep.start()
    lax.fori_loop(groups + 1, half, late, 0)

    for stream, h in flows:
        buf = (red_f, red_b)[stream]
        total = part(stream, h, me)
        for way in (1 - h, h):
            last = hops[h][way]
            reduce(stream, h, way, last - 1).wait_recv()
            total = total + buf[h, way, last].astype(F32)
        summed = total.astype(BF16).astype(F32)
        if stream == 0:
            own = gath_f[me, band(h)].astype(F32)
            fout_ref[band(h)] = (own + fweight_ref[...].astype(F32) * summed).astype(BF16)
        else:
            bout_ref[band(h)] = (gath_b[me, band(h)].astype(F32) + summed).astype(BF16)

    shift(0).wait_send()
    shift(1).wait_send()
    give().wait_send()
    give().wait_recv()
    keep.wait()
    for stream, h in flows:
        for way in range(2):
            first(stream, h, way).wait_send()
            reduce(stream, h, way, 0).wait_send()

            def drain(k, carry):
                gather_copy(stream, h, way, k, me).wait_send()
                reduce(stream, h, way, k).wait_send()
                return carry

            lax.fori_loop(1, hops[h][way], drain, 0)


def solution(mesh):
    ring = mesh.shape["expert"]
    sections = mesh.shape["pipe"]
    half = ring // 2

    def body(
        fwd_sent,
        fwd_route,
        fwd_weight,
        bwd_cot,
        bwd_route,
        bwd_weight,
        saved_gate,
        saved_up,
        gate_weight,
        up_weight,
        down_weight,
    ):
        rows, width = fwd_sent.shape[1:]
        units, model = gate_weight.shape[1:]
        dma = pltpu.SemaphoreType.DMA
        vmem = pl.BlockSpec(memory_space=pltpu.VMEM)
        anywhere = pl.BlockSpec(memory_space=pl.ANY)
        outs = pl.pallas_call(
            functools.partial(kernel, ring, sections),
            out_shape=(
                jax.ShapeDtypeStruct((width, rows), BF16),
                jax.ShapeDtypeStruct((width, rows), BF16),
                jax.ShapeDtypeStruct((units // 2, model), F32),
                jax.ShapeDtypeStruct((units // 2, model), F32),
            ),
            in_specs=[vmem] * 8 + [anywhere] * 3,
            out_specs=(vmem,) * 2 + (anywhere,) * 2,
            scratch_shapes=[
                pltpu.VMEM((units, model), BF16),
                pltpu.VMEM((units, model), BF16),
                pltpu.VMEM((units, model), BF16),
                pltpu.VMEM((ring, width, rows), BF16),
                pltpu.VMEM((ring, width, rows), BF16),
                pltpu.VMEM((2, 2, half + 1, width // 2, rows), BF16),
                pltpu.VMEM((2, 2, half + 1, width // 2, rows), BF16),
                pltpu.VMEM((ring, 2 * units, width), BF16),
                pltpu.VMEM((ring, units, width), BF16),
                pltpu.VMEM((ring, width, 2 * units), BF16),
                pltpu.VMEM((ring, width, units), BF16),
                pltpu.VMEM((2 * units, rows), F32),
                pltpu.VMEM((units, rows), F32),
                pltpu.VMEM((units, rows), F32),
                pltpu.VMEM((units, rows), F32),
                pltpu.VMEM((units, rows), BF16),
                pltpu.VMEM((units, rows), BF16),
                pltpu.VMEM((2 * units, rows), BF16),
                pltpu.VMEM((units, model), F32),
                dma((3,)),
                dma,
                dma((2,)),
                dma((2,)),
            ]
            + [dma((2, 2, 2, half))] * 4
            + [dma, dma],
            compiler_params=pltpu.CompilerParams(
                collective_id=0, has_side_effects=True, vmem_limit_bytes=56 * 1024 * 1024
            ),
        )(
            fwd_sent[0].T,
            fwd_route[0].T,
            fwd_weight[0].T,
            bwd_cot[0].T,
            bwd_route[0].T,
            bwd_weight[0].T,
            saved_gate[0, 0].T,
            saved_up[0, 0].T,
            gate_weight[0],
            up_weight[0],
            down_weight[0],
        )
        return outs[0].T[None], outs[1].T[None], (outs[2] + outs[3])[None]

    in_specs = (
        P("pipe", "dp", "expert"),
        P("pipe", "dp", None),
        P("pipe", "dp", None),
        P("pipe", "dp", "expert"),
        P("pipe", "dp", None),
        P("pipe", "dp", None),
        P("pipe", "dp", None, "expert"),
        P("pipe", "dp", None, "expert"),
        P("pipe", "expert", None),
        P("pipe", "expert", None),
        P("pipe", "expert", None),
    )
    out_specs = (
        P("pipe", "dp", "expert"),
        P("pipe", "dp", "expert"),
        P("pipe", ("expert", "dp"), None),
    )
    return jax.shard_map(body, mesh=mesh, in_specs=in_specs, out_specs=out_specs, check_vma=False)
```

```python
import functools

import jax
import jax.numpy as jnp
from jax import lax
from jax.experimental import pallas as pl
from jax.experimental.pallas import tpu as pltpu
from jax.sharding import PartitionSpec as P

EXPERTS = 2
LANES = 128
GROUP = 4
MESH = pl.DeviceIdType.MESH
BY_UNITS = (((1,), (1,)), ((), ()))
F32 = jnp.float32
BF16 = jnp.bfloat16


def dot(a, b):
    return jnp.dot(a, b, preferred_element_type=F32)


def dot_t(a, b):
    return lax.dot_general(a, b, BY_UNITS, preferred_element_type=F32)


def kernel(
    ring,
    sections,
    x_ref,
    froute_hbm,
    fweight_hbm,
    c_ref,
    broute_hbm,
    bweight_hbm,
    sgate_hbm,
    sup_hbm,
    wg_hbm,
    wu_hbm,
    wd_hbm,
    fout_ref,
    bout_ref,
    own_ref,
    peer_ref,
    broute_ref,
    sgate_ref,
    sup_ref,
    bweight_ref,
    froute_ref,
    fweight_ref,
    wg_ref,
    wu_ref,
    wd_ref,
    result,
    gath_f,
    gath_b,
    red_f,
    red_b,
    wgu,
    wdn,
    wgu_t,
    wdn_t,
    acc_f,
    acc_b,
    coef_g,
    coef_u,
    hbt,
    hid,
    dgu,
    dg,
    load_sem,
    keep_sem,
    out_sem,
    pipe_send,
    pipe_recv,
    gs,
    gr,
    rs,
    rr,
    dp_send,
    dp_recv,
):
    width, rows = x_ref.shape
    units = wg_hbm.shape[0]
    capacity = sgate_hbm.shape[1]
    half = ring // 2
    groups = ring // GROUP
    me = lax.axis_index("expert")
    section = lax.axis_index("pipe")
    replica = lax.axis_index("dp")
    right, left = lax.rem(me + 1, ring), lax.rem(me + ring - 1, ring)
    ahead, behind = lax.rem(section + 1, sections), lax.rem(section + sections - 1, sections)
    peer = 1 - replica
    expert = me // (ring // EXPERTS)

    part_width = width // 2
    hops = ((half, half - 1), (half - 1, half))
    flows = [(stream, h) for h in range(2) for stream in range(2)]
    sides = (right, left)
    stage = (ahead, behind)

    barrier = pltpu.get_barrier_semaphore()
    partners = [{"expert": right}, {"expert": left}, {"dp": peer}]
    for section_to in stage:
        partners.append({"pipe": section_to})
        partners += [{"pipe": section_to, "expert": side} for side in sides]
    for partner in partners:
        pl.semaphore_signal(barrier, inc=1, device_id=partner, device_id_type=MESH)
    loads = [
        pltpu.make_async_copy(hbm, ref, load_sem.at[i])
        for i, (hbm, ref) in enumerate(
            (
                (broute_hbm, broute_ref),
                (sgate_hbm, sgate_ref),
                (sup_hbm, sup_ref),
                (bweight_hbm, bweight_ref),
                (froute_hbm, froute_ref),
                (fweight_hbm, fweight_ref),
                (wg_hbm, wg_ref),
                (wu_hbm, wu_ref),
                (wd_hbm, wd_ref),
            )
        )
    ]
    for load in loads:
        load.start()
    pl.semaphore_wait(barrier, len(partners))

    def band(h):
        return pl.ds(h * part_width, part_width)

    def shift(stream):
        return pltpu.make_async_remote_copy(
            src_ref=(x_ref, c_ref)[stream],
            dst_ref=(gath_f, gath_b)[stream].at[me],
            send_sem=pipe_send.at[stream],
            recv_sem=pipe_recv.at[stream],
            device_id={"pipe": stage[stream]},
            device_id_type=MESH,
        )

    def first(stream, h, way):
        return pltpu.make_async_remote_copy(
            src_ref=(x_ref, c_ref)[stream].at[band(h)],
            dst_ref=(gath_f, gath_b)[stream].at[me, band(h)],
            send_sem=gs.at[stream, h, way, 0],
            recv_sem=gr.at[stream, h, way, 0],
            device_id={"pipe": stage[stream], "expert": sides[way]},
            device_id_type=MESH,
        )

    for stream, h in flows:
        for way in range(2):
            first(stream, h, way).start()
    for stream in range(2):
        shift(stream).start()

    for load in loads:
        load.wait()

    def split_weights(g):
        columns = pl.ds(pl.multiple_of(g * (GROUP * width), LANES), GROUP * width)
        both = jnp.concatenate([wg_ref[:, columns], wu_ref[:, columns]], axis=0)
        down = wd_ref[:, columns]
        for z in range(GROUP):
            piece = both[:, z * width : (z + 1) * width]
            wgu[GROUP * g + z] = piece
            wgu_t[GROUP * g + z] = jnp.transpose(piece)
            piece = down[:, z * width : (z + 1) * width]
            wdn[GROUP * g + z] = piece
            wdn_t[GROUP * g + z] = jnp.transpose(piece)

    def gather_copy(stream, h, way, k, shard):
        piece = (gath_f, gath_b)[stream].at[shard, band(h)]
        return pltpu.make_async_remote_copy(
            src_ref=piece,
            dst_ref=piece,
            send_sem=gs.at[stream, h, way, k],
            recv_sem=gr.at[stream, h, way, k],
            device_id={"expert": sides[way]},
            device_id_type=MESH,
        )

    def source(way, k):
        return lax.rem(me + ring - 1 - k, ring) if way == 0 else lax.rem(me + 1 + k, ring)

    def arrived(stream, h, way, k):
        gather_copy(stream, h, way, k, source(way, k)).wait_recv()

    def forward(stream, h, way, k):
        return gather_copy(stream, h, way, k + 1, source(way, k))

    bweight = bweight_ref[...].astype(F32)

    def use_f(shard):
        acc_f[...] += dot(wgu[shard], gath_f[shard])

    def use_b(shard):
        cot = (gath_b[shard].astype(F32) * bweight).astype(BF16)
        acc_b[...] += dot(wdn[shard], cot)

    acc_f[...] = jnp.zeros_like(acc_f)
    acc_b[...] = jnp.zeros_like(acc_b)

    before = (
        lax.broadcasted_iota(jnp.int32, (rows, rows), 0)
        < lax.broadcasted_iota(jnp.int32, (rows, rows), 1)
    ).astype(F32).astype(BF16)
    named = jnp.broadcast_to((broute_ref[...] == expert).astype(F32), (capacity, rows))
    slot = dot(named.astype(BF16), before)
    column = lax.broadcasted_iota(jnp.int32, (capacity, rows), 0).astype(F32)
    place = jnp.where(slot == column, named, 0.0).astype(BF16)
    gate_b = dot(sgate_ref[...], place)
    upper_b = dot(sup_ref[...], place)
    sig = jax.nn.sigmoid(gate_b)
    coef_g[...] = upper_b * sig * (1.0 + gate_b * (1.0 - sig))
    coef_u[...] = gate_b * sig
    hbt[...] = (gate_b * sig * upper_b).astype(BF16)

    def pass_on(stream, h, k):
        for way in range(2):
            arrived(stream, h, way, k)
            if hops[h][way] == half:
                forward(stream, h, way, k).start()
            else:

                @pl.when(k < half - 2)
                def _():
                    forward(stream, h, way, k).start()

    def use(k):
        for way in range(2):
            use_f(source(way, k))
            use_b(source(way, k))

    both = 2 - groups % 2
    opening = groups // both

    def gather_first(k, carry):
        for stream, h in flows:
            pass_on(stream, h, k)
            if stream == 1 and h < both:
                split_weights(both * k + h)
        return carry

    def gather_rest(k, carry):
        for stream, h in flows:
            pass_on(stream, h, k)

        @pl.when(k < 2 * opening)
        def _():
            use(k - opening)

        use(k)
        return carry

    lax.fori_loop(0, opening, gather_first, 0)
    shift(0).wait_recv()
    use_f(me)
    shift(1).wait_recv()
    use_b(me)
    lax.fori_loop(opening, half - 1, gather_rest, 0)
    for k in range(half - 1 - opening, opening):
        use(k)
    for h in range(2):
        arrived(0, h, h, half - 1)
    use_f(source(0, half - 1))
    gate = acc_f[:units]
    upper = acc_f[units:]
    hid[...] = jnp.where(
        froute_ref[...] == expert, gate * jax.nn.sigmoid(gate) * upper, 0.0
    ).astype(BF16)

    def part(stream, h, shard):
        if stream == 0:
            return dot(wdn_t[shard, band(h)], hid[...])
        return dot(wgu_t[shard, band(h)], dgu[...])

    def reduce(stream, h, way, k):
        buf = (red_f, red_b)[stream]
        return pltpu.make_async_remote_copy(
            src_ref=buf.at[h, way, k],
            dst_ref=buf.at[h, way, k + 1],
            send_sem=rs.at[stream, h, way, k],
            recv_sem=rr.at[stream, h, way, k],
            device_id={"expert": sides[way]},
            device_id_type=MESH,
        )

    def target(h, way, k):
        ahead_by = hops[h][way] - k
        return lax.rem(me + (ahead_by if way == 0 else ring - ahead_by), ring)

    def begin(stream):
        for h in range(2):
            for way in range(2):
                (red_f, red_b)[stream][h, way, 0] = part(stream, h, target(h, way, 0)).astype(BF16)
                reduce(stream, h, way, 0).start()

    begin(0)
    for h in range(2):
        arrived(1, h, h, half - 1)
    use_b(source(0, half - 1))
    d_hidden = acc_b[...]
    dgu[:units] = (d_hidden * coef_g[...]).astype(BF16)
    dgu[units:] = (d_hidden * coef_u[...]).astype(BF16)
    begin(1)

    def down_piece(g):
        raw = gath_b[pl.ds(GROUP * g, GROUP)].reshape(GROUP * width, rows)
        shards = (raw.astype(F32) * bweight).astype(BF16)
        start = pl.multiple_of(g * (GROUP * width), LANES)
        dg[:, pl.ds(start, GROUP * width)] = dot_t(hbt[...], shards)

    def relay(stream, h, way, k):
        buf = (red_f, red_b)[stream]
        term = part(stream, h, target(h, way, k))
        reduce(stream, h, way, k - 1).wait_recv()
        buf[h, way, k] = (buf[h, way, k].astype(F32) + term).astype(BF16)
        reduce(stream, h, way, k).start()

    def reduce_step(k):
        for stream, h in flows:
            for way in range(2):
                if hops[h][way] == half:
                    relay(stream, h, way, k)
                else:

                    @pl.when(k < half - 1)
                    def _():
                        relay(stream, h, way, k)

    def early(k, carry):
        reduce_step(k)
        down_piece(k - 1)
        return carry

    def late(k, carry):
        reduce_step(k)
        return carry

    def give():
        return pltpu.make_async_remote_copy(
            src_ref=dg.at[pl.ds(pl.multiple_of(peer * (units // 2), 8), units // 2)],
            dst_ref=peer_ref,
            send_sem=dp_send,
            recv_sem=dp_recv,
            device_id={"dp": peer},
            device_id_type=MESH,
        )

    mine_rows = pl.ds(pl.multiple_of(replica * (units // 2), 8), units // 2)
    keep = pltpu.make_async_copy(dg.at[mine_rows], own_ref, keep_sem)

    lax.fori_loop(1, groups + 1, early, 0)
    give().start()
    keep.start()
    lax.fori_loop(groups + 1, half, late, 0)

    def deliver(stream, h):
        return pltpu.make_async_copy(
            result.at[stream, band(h)],
            (fout_ref, bout_ref)[stream].at[band(h)],
            out_sem.at[stream, h],
        )

    for stream, h in flows:
        buf = (red_f, red_b)[stream]
        total = part(stream, h, me)
        for way in (1 - h, h):
            last = hops[h][way]
            reduce(stream, h, way, last - 1).wait_recv()
            total = total + buf[h, way, last].astype(F32)
        summed = total.astype(BF16).astype(F32)
        if stream == 0:
            own = gath_f[me, band(h)].astype(F32)
            out = own + fweight_ref[...].astype(F32) * summed
        else:
            out = gath_b[me, band(h)].astype(F32) + summed
        result[stream, band(h)] = out.astype(BF16)
        deliver(stream, h).start()

    shift(0).wait_send()
    shift(1).wait_send()
    give().wait_send()
    give().wait_recv()
    keep.wait()
    for stream, h in flows:
        for way in range(2):
            first(stream, h, way).wait_send()
            reduce(stream, h, way, 0).wait_send()

            def drain(k, carry):
                gather_copy(stream, h, way, k, me).wait_send()
                reduce(stream, h, way, k).wait_send()
                return carry

            lax.fori_loop(1, hops[h][way], drain, 0)
    for stream, h in flows:
        deliver(stream, h).wait()


def solution(mesh):
    ring = mesh.shape["expert"]
    sections = mesh.shape["pipe"]
    half = ring // 2

    def body(
        fwd_sent,
        fwd_route,
        fwd_weight,
        bwd_cot,
        bwd_route,
        bwd_weight,
        saved_gate,
        saved_up,
        gate_weight,
        up_weight,
        down_weight,
    ):
        rows, width = fwd_sent.shape[1:]
        units, model = gate_weight.shape[1:]
        dma = pltpu.SemaphoreType.DMA
        hbm = pl.BlockSpec(memory_space=pltpu.HBM)
        capacity = saved_gate.shape[2]
        outs = pl.pallas_call(
            functools.partial(kernel, ring, sections),
            out_shape=(
                jax.ShapeDtypeStruct((width, rows), BF16),
                jax.ShapeDtypeStruct((width, rows), BF16),
                jax.ShapeDtypeStruct((units // 2, model), F32),
                jax.ShapeDtypeStruct((units // 2, model), F32),
            ),
            in_specs=[hbm] * 11,
            out_specs=(hbm,) * 4,
            scratch_shapes=[
                pltpu.VMEM((1, rows), jnp.int32),
                pltpu.VMEM((units, capacity), BF16),
                pltpu.VMEM((units, capacity), BF16),
                pltpu.VMEM((1, rows), BF16),
                pltpu.VMEM((1, rows), jnp.int32),
                pltpu.VMEM((1, rows), BF16),
                pltpu.VMEM((units, model), BF16),
                pltpu.VMEM((units, model), BF16),
                pltpu.VMEM((units, model), BF16),
                pltpu.VMEM((2, width, rows), BF16),
                pltpu.VMEM((ring, width, rows), BF16),
                pltpu.VMEM((ring, width, rows), BF16),
                pltpu.VMEM((2, 2, half + 1, width // 2, rows), BF16),
                pltpu.VMEM((2, 2, half + 1, width // 2, rows), BF16),
                pltpu.VMEM((ring, 2 * units, width), BF16),
                pltpu.VMEM((ring, units, width), BF16),
                pltpu.VMEM((ring, width, 2 * units), BF16),
                pltpu.VMEM((ring, width, units), BF16),
                pltpu.VMEM((2 * units, rows), F32),
                pltpu.VMEM((units, rows), F32),
                pltpu.VMEM((units, rows), F32),
                pltpu.VMEM((units, rows), F32),
                pltpu.VMEM((units, rows), BF16),
                pltpu.VMEM((units, rows), BF16),
                pltpu.VMEM((2 * units, rows), BF16),
                pltpu.VMEM((units, model), F32),
                dma((9,)),
                dma,
                dma((2, 2)),
                dma((2,)),
                dma((2,)),
            ]
            + [dma((2, 2, 2, half))] * 4
            + [dma, dma],
            compiler_params=pltpu.CompilerParams(
                collective_id=0, has_side_effects=True, vmem_limit_bytes=56 * 1024 * 1024
            ),
        )(
            fwd_sent[0].T,
            fwd_route[0].T,
            fwd_weight[0].T,
            bwd_cot[0].T,
            bwd_route[0].T,
            bwd_weight[0].T,
            saved_gate[0, 0].T,
            saved_up[0, 0].T,
            gate_weight[0],
            up_weight[0],
            down_weight[0],
        )
        return outs[0].T[None], outs[1].T[None], (outs[2] + outs[3])[None]

    in_specs = (
        P("pipe", "dp", "expert"),
        P("pipe", "dp", None),
        P("pipe", "dp", None),
        P("pipe", "dp", "expert"),
        P("pipe", "dp", None),
        P("pipe", "dp", None),
        P("pipe", "dp", None, "expert"),
        P("pipe", "dp", None, "expert"),
        P("pipe", "expert", None),
        P("pipe", "expert", None),
        P("pipe", "expert", None),
    )
    out_specs = (
        P("pipe", "dp", "expert"),
        P("pipe", "dp", "expert"),
        P("pipe", ("expert", "dp"), None),
    )
    return jax.shard_map(body, mesh=mesh, in_specs=in_specs, out_specs=out_specs, check_vma=False)
```

```python
import functools

import jax
import jax.numpy as jnp
from jax import lax
from jax.experimental import pallas as pl
from jax.experimental.pallas import tpu as pltpu
from jax.sharding import PartitionSpec as P

EXPERTS = 2
LANES = 128
GROUP = 4
MESH = pl.DeviceIdType.MESH
BY_UNITS = (((1,), (1,)), ((), ()))
F32 = jnp.float32
BF16 = jnp.bfloat16


def dot(a, b):
    return jnp.dot(a, b, preferred_element_type=F32)


def dot_t(a, b):
    return lax.dot_general(a, b, BY_UNITS, preferred_element_type=F32)


def kernel(
    ring,
    sections,
    x_ref,
    froute_hbm,
    fweight_hbm,
    c_ref,
    broute_hbm,
    bweight_hbm,
    sgate_hbm,
    sup_hbm,
    wg_hbm,
    wu_hbm,
    wd_hbm,
    fout_ref,
    bout_ref,
    dgrad_ref,
    broute_ref,
    sgate_ref,
    sup_ref,
    bweight_ref,
    froute_ref,
    fweight_ref,
    wg_ref,
    wu_ref,
    wd_ref,
    result,
    gath_f,
    gath_b,
    red_f,
    red_b,
    wgu,
    wdn,
    wgu_t,
    wdn_t,
    acc_f,
    acc_b,
    coef_g,
    coef_u,
    hbt,
    hid,
    dgu,
    dg,
    dg_in,
    load_sem,
    keep_sem,
    out_sem,
    pipe_send,
    pipe_recv,
    gs,
    gr,
    rs,
    rr,
    dp_send,
    dp_recv,
):
    width, rows = x_ref.shape
    units = wg_hbm.shape[0]
    capacity = sgate_hbm.shape[1]
    half = ring // 2
    groups = ring // GROUP
    me = lax.axis_index("expert")
    section = lax.axis_index("pipe")
    replica = lax.axis_index("dp")
    right, left = lax.rem(me + 1, ring), lax.rem(me + ring - 1, ring)
    ahead, behind = lax.rem(section + 1, sections), lax.rem(section + sections - 1, sections)
    peer = 1 - replica
    expert = me // (ring // EXPERTS)

    part_width = width // 2
    hops = ((half, half - 1), (half - 1, half))
    flows = [(stream, h) for stream in range(2) for h in range(2)]
    sides = (right, left)
    stage = (ahead, behind)

    barrier = pltpu.get_barrier_semaphore()
    partners = [{"expert": right}, {"expert": left}, {"dp": peer}]
    for section_to in stage:
        partners.append({"pipe": section_to})
        partners += [{"pipe": section_to, "expert": side} for side in sides]
    for partner in partners:
        pl.semaphore_signal(barrier, inc=1, device_id=partner, device_id_type=MESH)
    loads = [
        pltpu.make_async_copy(hbm, ref, load_sem.at[i])
        for i, (hbm, ref) in enumerate(
            (
                (broute_hbm, broute_ref),
                (sgate_hbm, sgate_ref),
                (sup_hbm, sup_ref),
                (bweight_hbm, bweight_ref),
                (froute_hbm, froute_ref),
                (fweight_hbm, fweight_ref),
                (wg_hbm, wg_ref),
                (wu_hbm, wu_ref),
                (wd_hbm, wd_ref),
            )
        )
    ]
    for load in loads:
        load.start()
    pl.semaphore_wait(barrier, len(partners))

    def band(h):
        return pl.ds(h * part_width, part_width)

    def shift(stream):
        return pltpu.make_async_remote_copy(
            src_ref=(x_ref, c_ref)[stream],
            dst_ref=(gath_f, gath_b)[stream].at[me],
            send_sem=pipe_send.at[stream],
            recv_sem=pipe_recv.at[stream],
            device_id={"pipe": stage[stream]},
            device_id_type=MESH,
        )

    def first(stream, h, way):
        return pltpu.make_async_remote_copy(
            src_ref=(x_ref, c_ref)[stream].at[band(h)],
            dst_ref=(gath_f, gath_b)[stream].at[me, band(h)],
            send_sem=gs.at[stream, h, way, 0],
            recv_sem=gr.at[stream, h, way, 0],
            device_id={"pipe": stage[stream], "expert": sides[way]},
            device_id_type=MESH,
        )

    for stream, h in flows:
        for way in range(2):
            first(stream, h, way).start()
    for stream in range(2):
        shift(stream).start()

    for load in loads:
        load.wait()

    def split_weights(g):
        columns = pl.ds(pl.multiple_of(g * (GROUP * width), LANES), GROUP * width)
        both = jnp.concatenate([wg_ref[:, columns], wu_ref[:, columns]], axis=0)
        down = wd_ref[:, columns]
        for z in range(GROUP):
            piece = both[:, z * width : (z + 1) * width]
            wgu[GROUP * g + z] = piece
            wgu_t[GROUP * g + z] = jnp.transpose(piece)
            piece = down[:, z * width : (z + 1) * width]
            wdn[GROUP * g + z] = piece
            wdn_t[GROUP * g + z] = jnp.transpose(piece)

    def gather_copy(stream, h, way, k, shard):
        piece = (gath_f, gath_b)[stream].at[shard, band(h)]
        return pltpu.make_async_remote_copy(
            src_ref=piece,
            dst_ref=piece,
            send_sem=gs.at[stream, h, way, k],
            recv_sem=gr.at[stream, h, way, k],
            device_id={"expert": sides[way]},
            device_id_type=MESH,
        )

    def source(way, k):
        return lax.rem(me + ring - 1 - k, ring) if way == 0 else lax.rem(me + 1 + k, ring)

    def arrived(stream, h, way, k):
        gather_copy(stream, h, way, k, source(way, k)).wait_recv()

    def forward(stream, h, way, k):
        return gather_copy(stream, h, way, k + 1, source(way, k))

    bweight = bweight_ref[...].astype(F32)

    def use_f(shard):
        acc_f[...] += dot(wgu[shard], gath_f[shard])

    def use_b(shard):
        cot = (gath_b[shard].astype(F32) * bweight).astype(BF16)
        acc_b[...] += dot(wdn[shard], cot)

    acc_f[...] = jnp.zeros_like(acc_f)
    acc_b[...] = jnp.zeros_like(acc_b)

    before = (
        lax.broadcasted_iota(jnp.int32, (rows, rows), 0)
        < lax.broadcasted_iota(jnp.int32, (rows, rows), 1)
    ).astype(F32).astype(BF16)
    named = jnp.broadcast_to((broute_ref[...] == expert).astype(F32), (capacity, rows))
    slot = dot(named.astype(BF16), before)
    column = lax.broadcasted_iota(jnp.int32, (capacity, rows), 0).astype(F32)
    place = jnp.where(slot == column, named, 0.0).astype(BF16)
    gate_b = dot(sgate_ref[...], place)
    upper_b = dot(sup_ref[...], place)
    sig = jax.nn.sigmoid(gate_b)
    coef_g[...] = upper_b * sig * (1.0 + gate_b * (1.0 - sig))
    coef_u[...] = gate_b * sig
    hbt[...] = (gate_b * sig * upper_b).astype(BF16)

    def pass_on(stream, h, k):
        for way in range(2):
            arrived(stream, h, way, k)
            if hops[h][way] == half:
                forward(stream, h, way, k).start()
            else:

                @pl.when(k < half - 2)
                def _():
                    forward(stream, h, way, k).start()

    def use(k):
        for way in range(2):
            use_f(source(way, k))
            use_b(source(way, k))

    both = 2 - groups % 2
    opening = groups // both

    def gather_first(k, carry):
        for stream, h in flows:
            pass_on(stream, h, k)
            if stream == 1 and h < both:
                split_weights(both * k + h)
        return carry

    def gather_rest(k, carry):
        for stream, h in flows:
            pass_on(stream, h, k)

        @pl.when(k < 2 * opening)
        def _():
            use(k - opening)

        use(k)
        return carry

    lax.fori_loop(0, opening, gather_first, 0)
    shift(0).wait_recv()
    use_f(me)
    shift(1).wait_recv()
    use_b(me)
    lax.fori_loop(opening, half - 1, gather_rest, 0)
    for k in range(half - 1 - opening, opening):
        use(k)
    for h in range(2):
        arrived(0, h, h, half - 1)
    use_f(source(0, half - 1))
    gate = acc_f[:units]
    upper = acc_f[units:]
    hid[...] = jnp.where(
        froute_ref[...] == expert, gate * jax.nn.sigmoid(gate) * upper, 0.0
    ).astype(BF16)

    def part(stream, h, shard):
        if stream == 0:
            return dot(wdn_t[shard, band(h)], hid[...])
        return dot(wgu_t[shard, band(h)], dgu[...])

    def reduce(stream, h, way, k):
        buf = (red_f, red_b)[stream]
        return pltpu.make_async_remote_copy(
            src_ref=buf.at[h, way, k],
            dst_ref=buf.at[h, way, k + 1],
            send_sem=rs.at[stream, h, way, k],
            recv_sem=rr.at[stream, h, way, k],
            device_id={"expert": sides[way]},
            device_id_type=MESH,
        )

    def target(h, way, k):
        ahead_by = hops[h][way] - k
        return lax.rem(me + (ahead_by if way == 0 else ring - ahead_by), ring)

    def begin(stream):
        for h in range(2):
            for way in range(2):
                (red_f, red_b)[stream][h, way, 0] = part(stream, h, target(h, way, 0)).astype(BF16)
                reduce(stream, h, way, 0).start()

    begin(0)
    for h in range(2):
        arrived(1, h, h, half - 1)
    use_b(source(0, half - 1))
    d_hidden = acc_b[...]
    dgu[:units] = (d_hidden * coef_g[...]).astype(BF16)
    dgu[units:] = (d_hidden * coef_u[...]).astype(BF16)
    begin(1)

    def down_piece(g):
        raw = gath_b[pl.ds(GROUP * g, GROUP)].reshape(GROUP * width, rows)
        shards = (raw.astype(F32) * bweight).astype(BF16)
        start = pl.multiple_of(g * (GROUP * width), LANES)
        dg[:, pl.ds(start, GROUP * width)] = dot_t(hbt[...], shards)

    def relay(stream, h, way, k):
        buf = (red_f, red_b)[stream]
        term = part(stream, h, target(h, way, k))
        reduce(stream, h, way, k - 1).wait_recv()
        buf[h, way, k] = (buf[h, way, k].astype(F32) + term).astype(BF16)
        reduce(stream, h, way, k).start()

    def reduce_step(k):
        for stream, h in flows:
            for way in range(2):
                if hops[h][way] == half:
                    relay(stream, h, way, k)
                else:

                    @pl.when(k < half - 1)
                    def _():
                        relay(stream, h, way, k)

    def early(k, carry):
        reduce_step(k)
        down_piece(k - 1)
        return carry

    def late(k, carry):
        reduce_step(k)
        return carry

    def give():
        return pltpu.make_async_remote_copy(
            src_ref=dg.at[pl.ds(pl.multiple_of(peer * (units // 2), 8), units // 2)],
            dst_ref=dg_in,
            send_sem=dp_send,
            recv_sem=dp_recv,
            device_id={"dp": peer},
            device_id_type=MESH,
        )

    mine_rows = pl.ds(pl.multiple_of(replica * (units // 2), 8), units // 2)
    keep = pltpu.make_async_copy(dg_in, dgrad_ref, keep_sem)

    lax.fori_loop(1, groups + 1, early, 0)
    give().start()
    lax.fori_loop(groups + 1, half, late, 0)

    give().wait_recv()
    dg_in[...] += dg[mine_rows, :]
    keep.start()

    def deliver(stream, h):
        return pltpu.make_async_copy(
            result.at[stream, band(h)],
            (fout_ref, bout_ref)[stream].at[band(h)],
            out_sem.at[stream, h],
        )

    for stream, h in flows:
        buf = (red_f, red_b)[stream]
        total = part(stream, h, me)
        for way in (1 - h, h):
            last = hops[h][way]
            reduce(stream, h, way, last - 1).wait_recv()
            total = total + buf[h, way, last].astype(F32)
        summed = total.astype(BF16).astype(F32)
        if stream == 0:
            own = gath_f[me, band(h)].astype(F32)
            out = own + fweight_ref[...].astype(F32) * summed
        else:
            out = gath_b[me, band(h)].astype(F32) + summed
        result[stream, band(h)] = out.astype(BF16)
        deliver(stream, h).start()

    shift(0).wait_send()
    shift(1).wait_send()
    give().wait_send()
    keep.wait()
    for stream, h in flows:
        for way in range(2):
            first(stream, h, way).wait_send()
            reduce(stream, h, way, 0).wait_send()

            def drain(k, carry):
                gather_copy(stream, h, way, k, me).wait_send()
                reduce(stream, h, way, k).wait_send()
                return carry

            lax.fori_loop(1, hops[h][way], drain, 0)
    for stream, h in flows:
        deliver(stream, h).wait()


def hand_on(f_ref, b_ref, g_ref, fout_ref, bout_ref, gout_ref, sem, piece_sem):
    copies = []
    columns = g_ref.shape[1] // 2
    for i in range(g_ref.shape[0] // 8):
        for j in range(2):
            piece = (pl.ds(8 * i, 8), pl.ds(columns * j, columns))
            copies.append(
                pltpu.make_async_copy(g_ref.at[piece], gout_ref.at[piece], piece_sem.at[i, j])
            )
    copies.append(pltpu.make_async_copy(f_ref, fout_ref, sem.at[0]))
    copies.append(pltpu.make_async_copy(b_ref, bout_ref, sem.at[1]))
    for copy in copies:
        copy.start()
    for copy in copies:
        copy.wait()


def solution(mesh):
    ring = mesh.shape["expert"]
    sections = mesh.shape["pipe"]
    half = ring // 2

    def body(
        fwd_sent,
        fwd_route,
        fwd_weight,
        bwd_cot,
        bwd_route,
        bwd_weight,
        saved_gate,
        saved_up,
        gate_weight,
        up_weight,
        down_weight,
    ):
        rows, width = fwd_sent.shape[1:]
        units, model = gate_weight.shape[1:]
        dma = pltpu.SemaphoreType.DMA
        hbm = pl.BlockSpec(memory_space=pltpu.HBM)
        capacity = saved_gate.shape[2]
        outs = pl.pallas_call(
            functools.partial(kernel, ring, sections),
            out_shape=(
                jax.ShapeDtypeStruct((width, rows), BF16),
                jax.ShapeDtypeStruct((width, rows), BF16),
                jax.ShapeDtypeStruct((units // 2, model), F32),
            ),
            in_specs=[hbm] * 11,
            out_specs=(hbm,) * 3,
            scratch_shapes=[
                pltpu.VMEM((1, rows), jnp.int32),
                pltpu.VMEM((units, capacity), BF16),
                pltpu.VMEM((units, capacity), BF16),
                pltpu.VMEM((1, rows), BF16),
                pltpu.VMEM((1, rows), jnp.int32),
                pltpu.VMEM((1, rows), BF16),
                pltpu.VMEM((units, model), BF16),
                pltpu.VMEM((units, model), BF16),
                pltpu.VMEM((units, model), BF16),
                pltpu.VMEM((2, width, rows), BF16),
                pltpu.VMEM((ring, width, rows), BF16),
                pltpu.VMEM((ring, width, rows), BF16),
                pltpu.VMEM((2, 2, half + 1, width // 2, rows), BF16),
                pltpu.VMEM((2, 2, half + 1, width // 2, rows), BF16),
                pltpu.VMEM((ring, 2 * units, width), BF16),
                pltpu.VMEM((ring, units, width), BF16),
                pltpu.VMEM((ring, width, 2 * units), BF16),
                pltpu.VMEM((ring, width, units), BF16),
                pltpu.VMEM((2 * units, rows), F32),
                pltpu.VMEM((units, rows), F32),
                pltpu.VMEM((units, rows), F32),
                pltpu.VMEM((units, rows), F32),
                pltpu.VMEM((units, rows), BF16),
                pltpu.VMEM((units, rows), BF16),
                pltpu.VMEM((2 * units, rows), BF16),
                pltpu.VMEM((units, model), F32),
                pltpu.VMEM((units // 2, model), F32),
                dma((9,)),
                dma,
                dma((2, 2)),
                dma((2,)),
                dma((2,)),
            ]
            + [dma((2, 2, 2, half))] * 4
            + [dma, dma],
            compiler_params=pltpu.CompilerParams(
                collective_id=0, has_side_effects=True, vmem_limit_bytes=56 * 1024 * 1024
            ),
        )(
            fwd_sent[0].T,
            fwd_route[0].T,
            fwd_weight[0].T,
            bwd_cot[0].T,
            bwd_route[0].T,
            bwd_weight[0].T,
            saved_gate[0, 0].T,
            saved_up[0, 0].T,
            gate_weight[0],
            up_weight[0],
            down_weight[0],
        )
        outs = pl.pallas_call(
            hand_on,
            out_shape=tuple(jax.ShapeDtypeStruct(out.shape, out.dtype) for out in outs),
            in_specs=[hbm] * 3,
            out_specs=(hbm,) * 3,
            scratch_shapes=[dma((2,)), dma((units // 16, 2))],
        )(*outs)
        return outs[0].T[None], outs[1].T[None], outs[2][None]

    in_specs = (
        P("pipe", "dp", "expert"),
        P("pipe", "dp", None),
        P("pipe", "dp", None),
        P("pipe", "dp", "expert"),
        P("pipe", "dp", None),
        P("pipe", "dp", None),
        P("pipe", "dp", None, "expert"),
        P("pipe", "dp", None, "expert"),
        P("pipe", "expert", None),
        P("pipe", "expert", None),
        P("pipe", "expert", None),
    )
    out_specs = (
        P("pipe", "dp", "expert"),
        P("pipe", "dp", "expert"),
        P("pipe", ("expert", "dp"), None),
    )
    return jax.shard_map(body, mesh=mesh, in_specs=in_specs, out_specs=out_specs, check_vma=False)
```

```python
import functools

import jax
import jax.numpy as jnp
from jax import lax
from jax.experimental import pallas as pl
from jax.experimental.pallas import tpu as pltpu
from jax.sharding import PartitionSpec as P

EXPERTS = 2
LANES = 128
GROUP = 4
MESH = pl.DeviceIdType.MESH
BY_UNITS = (((1,), (1,)), ((), ()))
F32 = jnp.float32
BF16 = jnp.bfloat16


def dot(a, b):
    return jnp.dot(a, b, preferred_element_type=F32)


def dot_t(a, b):
    return lax.dot_general(a, b, BY_UNITS, preferred_element_type=F32)


def kernel(
    ring,
    sections,
    x_ref,
    froute_hbm,
    fweight_hbm,
    c_ref,
    broute_hbm,
    bweight_hbm,
    sgate_hbm,
    sup_hbm,
    wg_hbm,
    wu_hbm,
    wd_hbm,
    fout_ref,
    bout_ref,
    dgrad_ref,
    broute_ref,
    sgate_ref,
    sup_ref,
    bweight_ref,
    froute_ref,
    fweight_ref,
    wg_ref,
    wu_ref,
    wd_ref,
    result,
    gath_f,
    gath_b,
    red_f,
    red_b,
    wgu,
    wdn,
    wgu_t,
    wdn_t,
    acc_f,
    acc_b,
    coef_g,
    coef_u,
    hbt,
    hid,
    dgu,
    dg,
    dg_in,
    load_sem,
    keep_sem,
    out_sem,
    pipe_send,
    pipe_recv,
    gs,
    gr,
    rs,
    rr,
    dp_send,
    dp_recv,
):
    width, rows = x_ref.shape
    units = wg_hbm.shape[0]
    capacity = sgate_hbm.shape[1]
    half = ring // 2
    groups = ring // GROUP
    me = lax.axis_index("expert")
    section = lax.axis_index("pipe")
    replica = lax.axis_index("dp")
    right, left = lax.rem(me + 1, ring), lax.rem(me + ring - 1, ring)
    ahead, behind = lax.rem(section + 1, sections), lax.rem(section + sections - 1, sections)
    peer = 1 - replica
    expert = me // (ring // EXPERTS)

    part_width = width // 2
    hops = ((half, half - 1), (half - 1, half))
    flows = [(stream, h) for stream in range(2) for h in range(2)]
    sides = (right, left)
    stage = (ahead, behind)

    barrier = pltpu.get_barrier_semaphore()
    partners = [{"expert": right}, {"expert": left}, {"dp": peer}]
    for section_to in stage:
        partners.append({"pipe": section_to})
        partners += [{"pipe": section_to, "expert": side} for side in sides]
    for partner in partners:
        pl.semaphore_signal(barrier, inc=1, device_id=partner, device_id_type=MESH)
    loads = [
        pltpu.make_async_copy(hbm, ref, load_sem.at[i])
        for i, (hbm, ref) in enumerate(
            (
                (broute_hbm, broute_ref),
                (sgate_hbm, sgate_ref),
                (sup_hbm, sup_ref),
                (bweight_hbm, bweight_ref),
                (froute_hbm, froute_ref),
                (fweight_hbm, fweight_ref),
                (wg_hbm, wg_ref),
                (wu_hbm, wu_ref),
                (wd_hbm, wd_ref),
            )
        )
    ]
    for load in loads:
        load.start()
    pl.semaphore_wait(barrier, len(partners))

    def band(h):
        return pl.ds(h * part_width, part_width)

    def shift(stream):
        return pltpu.make_async_remote_copy(
            src_ref=(x_ref, c_ref)[stream],
            dst_ref=(gath_f, gath_b)[stream].at[me],
            send_sem=pipe_send.at[stream],
            recv_sem=pipe_recv.at[stream],
            device_id={"pipe": stage[stream]},
            device_id_type=MESH,
        )

    def first(stream, h, way):
        return pltpu.make_async_remote_copy(
            src_ref=(x_ref, c_ref)[stream].at[band(h)],
            dst_ref=(gath_f, gath_b)[stream].at[me, band(h)],
            send_sem=gs.at[stream, h, way, 0],
            recv_sem=gr.at[stream, h, way, 0],
            device_id={"pipe": stage[stream], "expert": sides[way]},
            device_id_type=MESH,
        )

    for stream, h in flows:
        for way in range(2):
            first(stream, h, way).start()
    for stream in range(2):
        shift(stream).start()

    for load in loads:
        load.wait()

    def split_weights(g):
        columns = pl.ds(pl.multiple_of(g * (GROUP * width), LANES), GROUP * width)
        both = jnp.concatenate([wg_ref[:, columns], wu_ref[:, columns]], axis=0)
        down = wd_ref[:, columns]
        for z in range(GROUP):
            piece = both[:, z * width : (z + 1) * width]
            wgu[GROUP * g + z] = piece
            wgu_t[GROUP * g + z] = jnp.transpose(piece)
            piece = down[:, z * width : (z + 1) * width]
            wdn[GROUP * g + z] = piece
            wdn_t[GROUP * g + z] = jnp.transpose(piece)

    def gather_copy(stream, h, way, k, shard):
        piece = (gath_f, gath_b)[stream].at[shard, band(h)]
        return pltpu.make_async_remote_copy(
            src_ref=piece,
            dst_ref=piece,
            send_sem=gs.at[stream, h, way, k],
            recv_sem=gr.at[stream, h, way, k],
            device_id={"expert": sides[way]},
            device_id_type=MESH,
        )

    def source(way, k):
        return lax.rem(me + ring - 1 - k, ring) if way == 0 else lax.rem(me + 1 + k, ring)

    def arrived(stream, h, way, k):
        gather_copy(stream, h, way, k, source(way, k)).wait_recv()

    def forward(stream, h, way, k):
        return gather_copy(stream, h, way, k + 1, source(way, k))

    bweight = bweight_ref[...].astype(F32)

    def use_f(shard):
        acc_f[...] += dot(wgu[shard], gath_f[shard])

    def use_b(shard):
        cot = (gath_b[shard].astype(F32) * bweight).astype(BF16)
        acc_b[...] += dot(wdn[shard], cot)

    acc_f[...] = jnp.zeros_like(acc_f)
    acc_b[...] = jnp.zeros_like(acc_b)

    before = (
        lax.broadcasted_iota(jnp.int32, (rows, rows), 0)
        < lax.broadcasted_iota(jnp.int32, (rows, rows), 1)
    ).astype(F32).astype(BF16)
    named = jnp.broadcast_to((broute_ref[...] == expert).astype(F32), (capacity, rows))
    slot = dot(named.astype(BF16), before)
    column = lax.broadcasted_iota(jnp.int32, (capacity, rows), 0).astype(F32)
    place = jnp.where(slot == column, named, 0.0).astype(BF16)
    gate_b = dot(sgate_ref[...], place)
    upper_b = dot(sup_ref[...], place)
    sig = jax.nn.sigmoid(gate_b)
    coef_g[...] = upper_b * sig * (1.0 + gate_b * (1.0 - sig))
    coef_u[...] = gate_b * sig
    hbt[...] = (gate_b * sig * upper_b).astype(BF16)

    def pass_on(stream, h, k):
        for way in range(2):
            arrived(stream, h, way, k)
            if hops[h][way] == half:
                forward(stream, h, way, k).start()
            else:

                @pl.when(k < half - 2)
                def _():
                    forward(stream, h, way, k).start()

    def use(k):
        for way in range(2):
            use_f(source(way, k))
            use_b(source(way, k))

    both = 2 - groups % 2
    opening = groups // both

    def gather_first(k, carry):
        for stream, h in flows:
            pass_on(stream, h, k)
            if stream == 1 and h < both:
                split_weights(both * k + h)
        return carry

    def gather_rest(k, carry):
        for stream, h in flows:
            pass_on(stream, h, k)

        @pl.when(k < 2 * opening)
        def _():
            use(k - opening)

        use(k)
        return carry

    lax.fori_loop(0, opening, gather_first, 0)
    shift(0).wait_recv()
    use_f(me)
    shift(1).wait_recv()
    use_b(me)
    lax.fori_loop(opening, half - 1, gather_rest, 0)
    for k in range(half - 1 - opening, opening):
        use(k)
    for h in range(2):
        arrived(0, h, h, half - 1)
    use_f(source(0, half - 1))
    gate = acc_f[:units]
    upper = acc_f[units:]
    hid[...] = jnp.where(
        froute_ref[...] == expert, gate * jax.nn.sigmoid(gate) * upper, 0.0
    ).astype(BF16)

    def part(stream, h, shard):
        if stream == 0:
            return dot(wdn_t[shard, band(h)], hid[...])
        return dot(wgu_t[shard, band(h)], dgu[...])

    def reduce(stream, h, way, k):
        buf = (red_f, red_b)[stream]
        return pltpu.make_async_remote_copy(
            src_ref=buf.at[h, way, k],
            dst_ref=buf.at[h, way, k + 1],
            send_sem=rs.at[stream, h, way, k],
            recv_sem=rr.at[stream, h, way, k],
            device_id={"expert": sides[way]},
            device_id_type=MESH,
        )

    def target(h, way, k):
        ahead_by = hops[h][way] - k
        return lax.rem(me + (ahead_by if way == 0 else ring - ahead_by), ring)

    def begin(stream):
        for h in range(2):
            for way in range(2):
                (red_f, red_b)[stream][h, way, 0] = part(stream, h, target(h, way, 0)).astype(BF16)
                reduce(stream, h, way, 0).start()

    begin(0)
    for h in range(2):
        arrived(1, h, h, half - 1)
    use_b(source(0, half - 1))
    d_hidden = acc_b[...]
    dgu[:units] = (d_hidden * coef_g[...]).astype(BF16)
    dgu[units:] = (d_hidden * coef_u[...]).astype(BF16)
    begin(1)

    def down_piece(g):
        raw = gath_b[pl.ds(GROUP * g, GROUP)].reshape(GROUP * width, rows)
        shards = (raw.astype(F32) * bweight).astype(BF16)
        start = pl.multiple_of(g * (GROUP * width), LANES)
        dg[:, pl.ds(start, GROUP * width)] = dot_t(hbt[...], shards)

    def relay(stream, h, way, k):
        buf = (red_f, red_b)[stream]
        term = part(stream, h, target(h, way, k))
        reduce(stream, h, way, k - 1).wait_recv()
        buf[h, way, k] = (buf[h, way, k].astype(F32) + term).astype(BF16)
        reduce(stream, h, way, k).start()

    def reduce_step(k):
        for stream, h in flows:
            for way in range(2):
                if hops[h][way] == half:
                    relay(stream, h, way, k)
                else:

                    @pl.when(k < half - 1)
                    def _():
                        relay(stream, h, way, k)

    def early(k, carry):
        reduce_step(k)
        down_piece(k - 1)
        return carry

    def late(k, carry):
        reduce_step(k)
        return carry

    def give():
        return pltpu.make_async_remote_copy(
            src_ref=dg.at[pl.ds(pl.multiple_of(peer * (units // 2), 8), units // 2)],
            dst_ref=dg_in,
            send_sem=dp_send,
            recv_sem=dp_recv,
            device_id={"dp": peer},
            device_id_type=MESH,
        )

    mine_rows = pl.ds(pl.multiple_of(replica * (units // 2), 8), units // 2)
    keep = pltpu.make_async_copy(dg_in, dgrad_ref, keep_sem)

    lax.fori_loop(1, groups + 1, early, 0)
    give().start()
    lax.fori_loop(groups + 1, half, late, 0)

    give().wait_recv()
    dg_in[...] += dg[mine_rows, :]
    keep.start()

    def deliver(stream, h):
        return pltpu.make_async_copy(
            result.at[stream, band(h)],
            (fout_ref, bout_ref)[stream].at[band(h)],
            out_sem.at[stream, h],
        )

    for stream, h in flows:
        buf = (red_f, red_b)[stream]
        total = part(stream, h, me)
        for way in (1 - h, h):
            last = hops[h][way]
            reduce(stream, h, way, last - 1).wait_recv()
            total = total + buf[h, way, last].astype(F32)
        summed = total.astype(BF16).astype(F32)
        if stream == 0:
            own = gath_f[me, band(h)].astype(F32)
            out = own + fweight_ref[...].astype(F32) * summed
        else:
            out = gath_b[me, band(h)].astype(F32) + summed
        result[stream, band(h)] = out.astype(BF16)
        deliver(stream, h).start()

    shift(0).wait_send()
    shift(1).wait_send()
    give().wait_send()
    keep.wait()
    for stream, h in flows:
        for way in range(2):
            first(stream, h, way).wait_send()
            reduce(stream, h, way, 0).wait_send()

            def drain(k, carry):
                gather_copy(stream, h, way, k, me).wait_send()
                reduce(stream, h, way, k).wait_send()
                return carry

            lax.fori_loop(1, hops[h][way], drain, 0)
    for stream, h in flows:
        deliver(stream, h).wait()


def hand_on(f_ref, b_ref, g_ref, fout_ref, bout_ref, gout_ref, f_held, b_held, g_held, sem, piece_sem):
    pieces = []
    columns = g_ref.shape[1] // 2
    for i in range(g_ref.shape[0] // 8):
        for j in range(2):
            piece = (pl.ds(8 * i, 8), pl.ds(columns * j, columns))
            pieces.append((g_ref.at[piece], g_held.at[piece], gout_ref.at[piece], piece_sem.at[i, j]))
    pieces.append((f_ref, f_held, fout_ref, sem.at[0]))
    pieces.append((b_ref, b_held, bout_ref, sem.at[1]))
    come = [pltpu.make_async_copy(src, held, own.at[0]) for src, held, _, own in pieces]
    go = [pltpu.make_async_copy(held, dst, own.at[1]) for _, held, dst, own in pieces]
    for copy in come:
        copy.start()
    for arrive, leave in zip(come, go):
        arrive.wait()
        leave.start()
    for copy in go:
        copy.wait()


def solution(mesh):
    ring = mesh.shape["expert"]
    sections = mesh.shape["pipe"]
    half = ring // 2

    def body(
        fwd_sent,
        fwd_route,
        fwd_weight,
        bwd_cot,
        bwd_route,
        bwd_weight,
        saved_gate,
        saved_up,
        gate_weight,
        up_weight,
        down_weight,
    ):
        rows, width = fwd_sent.shape[1:]
        units, model = gate_weight.shape[1:]
        dma = pltpu.SemaphoreType.DMA
        hbm = pl.BlockSpec(memory_space=pltpu.HBM)
        capacity = saved_gate.shape[2]
        outs = pl.pallas_call(
            functools.partial(kernel, ring, sections),
            out_shape=(
                jax.ShapeDtypeStruct((width, rows), BF16),
                jax.ShapeDtypeStruct((width, rows), BF16),
                jax.ShapeDtypeStruct((units // 2, model), F32),
            ),
            in_specs=[hbm] * 11,
            out_specs=(hbm,) * 3,
            scratch_shapes=[
                pltpu.VMEM((1, rows), jnp.int32),
                pltpu.VMEM((units, capacity), BF16),
                pltpu.VMEM((units, capacity), BF16),
                pltpu.VMEM((1, rows), BF16),
                pltpu.VMEM((1, rows), jnp.int32),
                pltpu.VMEM((1, rows), BF16),
                pltpu.VMEM((units, model), BF16),
                pltpu.VMEM((units, model), BF16),
                pltpu.VMEM((units, model), BF16),
                pltpu.VMEM((2, width, rows), BF16),
                pltpu.VMEM((ring, width, rows), BF16),
                pltpu.VMEM((ring, width, rows), BF16),
                pltpu.VMEM((2, 2, half + 1, width // 2, rows), BF16),
                pltpu.VMEM((2, 2, half + 1, width // 2, rows), BF16),
                pltpu.VMEM((ring, 2 * units, width), BF16),
                pltpu.VMEM((ring, units, width), BF16),
                pltpu.VMEM((ring, width, 2 * units), BF16),
                pltpu.VMEM((ring, width, units), BF16),
                pltpu.VMEM((2 * units, rows), F32),
                pltpu.VMEM((units, rows), F32),
                pltpu.VMEM((units, rows), F32),
                pltpu.VMEM((units, rows), F32),
                pltpu.VMEM((units, rows), BF16),
                pltpu.VMEM((units, rows), BF16),
                pltpu.VMEM((2 * units, rows), BF16),
                pltpu.VMEM((units, model), F32),
                pltpu.VMEM((units // 2, model), F32),
                dma((9,)),
                dma,
                dma((2, 2)),
                dma((2,)),
                dma((2,)),
            ]
            + [dma((2, 2, 2, half))] * 4
            + [dma, dma],
            compiler_params=pltpu.CompilerParams(
                collective_id=0, has_side_effects=True, vmem_limit_bytes=56 * 1024 * 1024
            ),
        )(
            fwd_sent[0].T,
            fwd_route[0].T,
            fwd_weight[0].T,
            bwd_cot[0].T,
            bwd_route[0].T,
            bwd_weight[0].T,
            saved_gate[0, 0].T,
            saved_up[0, 0].T,
            gate_weight[0],
            up_weight[0],
            down_weight[0],
        )
        outs = pl.pallas_call(
            hand_on,
            out_shape=tuple(jax.ShapeDtypeStruct(out.shape, out.dtype) for out in outs),
            in_specs=[hbm] * 3,
            out_specs=(hbm,) * 3,
            scratch_shapes=[pltpu.VMEM(out.shape, out.dtype) for out in outs]
            + [dma((2, 2)), dma((units // 16, 2, 2))],
        )(*outs)
        return outs[0].T[None], outs[1].T[None], outs[2][None]

    in_specs = (
        P("pipe", "dp", "expert"),
        P("pipe", "dp", None),
        P("pipe", "dp", None),
        P("pipe", "dp", "expert"),
        P("pipe", "dp", None),
        P("pipe", "dp", None),
        P("pipe", "dp", None, "expert"),
        P("pipe", "dp", None, "expert"),
        P("pipe", "expert", None),
        P("pipe", "expert", None),
        P("pipe", "expert", None),
    )
    out_specs = (
        P("pipe", "dp", "expert"),
        P("pipe", "dp", "expert"),
        P("pipe", ("expert", "dp"), None),
    )
    return jax.shard_map(body, mesh=mesh, in_specs=in_specs, out_specs=out_specs, check_vma=False)
```

```python
import functools

import jax
import jax.numpy as jnp
from jax import lax
from jax.experimental import pallas as pl
from jax.experimental.pallas import tpu as pltpu
from jax.sharding import PartitionSpec as P

EXPERTS = 2
LANES = 128
GROUP = 4
MESH = pl.DeviceIdType.MESH
BY_UNITS = (((1,), (1,)), ((), ()))
F32 = jnp.float32
BF16 = jnp.bfloat16


def dot(a, b):
    return jnp.dot(a, b, preferred_element_type=F32)


def dot_t(a, b):
    return lax.dot_general(a, b, BY_UNITS, preferred_element_type=F32)


def kernel(
    ring,
    sections,
    x_ref,
    froute_hbm,
    fweight_hbm,
    c_ref,
    broute_hbm,
    bweight_hbm,
    sgate_hbm,
    sup_hbm,
    wg_hbm,
    wu_hbm,
    wd_hbm,
    fout_ref,
    bout_ref,
    dgrad_ref,
    broute_ref,
    sgate_ref,
    sup_ref,
    bweight_ref,
    froute_ref,
    fweight_ref,
    wg_ref,
    wu_ref,
    wd_ref,
    result,
    gath_f,
    gath_b,
    red_f,
    red_b,
    wgu,
    wdn,
    wgu_t,
    wdn_t,
    acc_f,
    acc_b,
    coef_g,
    coef_u,
    hbt,
    hid,
    dgu,
    dg,
    dg_in,
    load_sem,
    keep_sem,
    out_sem,
    pipe_send,
    pipe_recv,
    gs,
    gr,
    rs,
    rr,
    dp_send,
    dp_recv,
):
    width, rows = x_ref.shape
    units = wg_hbm.shape[0]
    capacity = sgate_hbm.shape[1]
    half = ring // 2
    groups = ring // GROUP
    me = lax.axis_index("expert")
    section = lax.axis_index("pipe")
    replica = lax.axis_index("dp")
    right, left = lax.rem(me + 1, ring), lax.rem(me + ring - 1, ring)
    ahead, behind = lax.rem(section + 1, sections), lax.rem(section + sections - 1, sections)
    peer = 1 - replica
    expert = me // (ring // EXPERTS)

    part_width = width // 2
    hops = ((half, half - 1), (half - 1, half))
    flows = [(stream, h) for stream in range(2) for h in range(2)]
    sides = (right, left)
    stage = (ahead, behind)

    barrier = pltpu.get_barrier_semaphore()
    partners = [{"expert": right}, {"expert": left}, {"dp": peer}]
    for section_to in stage:
        partners.append({"pipe": section_to})
        partners += [{"pipe": section_to, "expert": side} for side in sides]
    for partner in partners:
        pl.semaphore_signal(barrier, inc=1, device_id=partner, device_id_type=MESH)
    loads = [
        pltpu.make_async_copy(hbm, ref, load_sem.at[i])
        for i, (hbm, ref) in enumerate(
            (
                (broute_hbm, broute_ref),
                (sgate_hbm, sgate_ref),
                (sup_hbm, sup_ref),
                (bweight_hbm, bweight_ref),
                (froute_hbm, froute_ref),
                (fweight_hbm, fweight_ref),
                (wg_hbm, wg_ref),
                (wu_hbm, wu_ref),
                (wd_hbm, wd_ref),
            )
        )
    ]
    for load in loads:
        load.start()
    pl.semaphore_wait(barrier, len(partners))

    def band(h):
        return pl.ds(h * part_width, part_width)

    def shift(stream):
        return pltpu.make_async_remote_copy(
            src_ref=(x_ref, c_ref)[stream],
            dst_ref=(gath_f, gath_b)[stream].at[me],
            send_sem=pipe_send.at[stream],
            recv_sem=pipe_recv.at[stream],
            device_id={"pipe": stage[stream]},
            device_id_type=MESH,
        )

    def first(stream, h, way):
        return pltpu.make_async_remote_copy(
            src_ref=(x_ref, c_ref)[stream].at[band(h)],
            dst_ref=(gath_f, gath_b)[stream].at[me, band(h)],
            send_sem=gs.at[stream, h, way, 0],
            recv_sem=gr.at[stream, h, way, 0],
            device_id={"pipe": stage[stream], "expert": sides[way]},
            device_id_type=MESH,
        )

    for stream, h in flows:
        for way in range(2):
            first(stream, h, way).start()
    for stream in range(2):
        shift(stream).start()

    for load in loads:
        load.wait()

    def split_weights(g):
        columns = pl.ds(pl.multiple_of(g * (GROUP * width), LANES), GROUP * width)
        both = jnp.concatenate([wg_ref[:, columns], wu_ref[:, columns]], axis=0)
        down = wd_ref[:, columns]
        for z in range(GROUP):
            piece = both[:, z * width : (z + 1) * width]
            wgu[GROUP * g + z] = piece
            wgu_t[GROUP * g + z] = jnp.transpose(piece)
            piece = down[:, z * width : (z + 1) * width]
            wdn[GROUP * g + z] = piece
            wdn_t[GROUP * g + z] = jnp.transpose(piece)

    def gather_copy(stream, h, way, k, shard):
        piece = (gath_f, gath_b)[stream].at[shard, band(h)]
        return pltpu.make_async_remote_copy(
            src_ref=piece,
            dst_ref=piece,
            send_sem=gs.at[stream, h, way, k],
            recv_sem=gr.at[stream, h, way, k],
            device_id={"expert": sides[way]},
            device_id_type=MESH,
        )

    def source(way, k):
        return lax.rem(me + ring - 1 - k, ring) if way == 0 else lax.rem(me + 1 + k, ring)

    def arrived(stream, h, way, k):
        gather_copy(stream, h, way, k, source(way, k)).wait_recv()

    def forward(stream, h, way, k):
        return gather_copy(stream, h, way, k + 1, source(way, k))

    bweight = bweight_ref[...].astype(F32)

    def use_f(shard):
        acc_f[...] += dot(wgu[shard], gath_f[shard])

    def use_b(shard):
        cot = (gath_b[shard].astype(F32) * bweight).astype(BF16)
        acc_b[...] += dot(wdn[shard], cot)

    acc_f[...] = jnp.zeros_like(acc_f)
    acc_b[...] = jnp.zeros_like(acc_b)

    before = (
        lax.broadcasted_iota(jnp.int32, (rows, rows), 0)
        < lax.broadcasted_iota(jnp.int32, (rows, rows), 1)
    ).astype(F32).astype(BF16)
    named = jnp.broadcast_to((broute_ref[...] == expert).astype(F32), (capacity, rows))
    slot = dot(named.astype(BF16), before)
    column = lax.broadcasted_iota(jnp.int32, (capacity, rows), 0).astype(F32)
    place = jnp.where(slot == column, named, 0.0).astype(BF16)
    gate_b = dot(sgate_ref[...], place)
    upper_b = dot(sup_ref[...], place)
    sig = jax.nn.sigmoid(gate_b)
    coef_g[...] = upper_b * sig * (1.0 + gate_b * (1.0 - sig))
    coef_u[...] = gate_b * sig
    hbt[...] = (gate_b * sig * upper_b).astype(BF16)

    def pass_on(stream, h, k):
        for way in range(2):
            arrived(stream, h, way, k)
            if hops[h][way] == half:
                forward(stream, h, way, k).start()
            else:

                @pl.when(k < half - 2)
                def _():
                    forward(stream, h, way, k).start()

    def use(k):
        for way in range(2):
            use_f(source(way, k))
            use_b(source(way, k))

    both = 2 - groups % 2
    opening = groups // both

    def gather_first(k, carry):
        for stream, h in flows:
            pass_on(stream, h, k)
            if stream == 1 and h < both:
                split_weights(both * k + h)
        return carry

    def gather_rest(k, carry):
        for stream, h in flows:
            pass_on(stream, h, k)

        @pl.when(k < 2 * opening)
        def _():
            use(k - opening)

        use(k)
        return carry

    lax.fori_loop(0, opening, gather_first, 0)
    shift(0).wait_recv()
    use_f(me)
    shift(1).wait_recv()
    use_b(me)
    lax.fori_loop(opening, half - 1, gather_rest, 0)
    for k in range(half - 1 - opening, opening):
        use(k)
    for h in range(2):
        arrived(0, h, h, half - 1)
    use_f(source(0, half - 1))
    gate = acc_f[:units]
    upper = acc_f[units:]
    hid[...] = jnp.where(
        froute_ref[...] == expert, gate * jax.nn.sigmoid(gate) * upper, 0.0
    ).astype(BF16)

    def part(stream, h, shard):
        if stream == 0:
            return dot(wdn_t[shard, band(h)], hid[...])
        return dot(wgu_t[shard, band(h)], dgu[...])

    def reduce(stream, h, way, k):
        buf = (red_f, red_b)[stream]
        return pltpu.make_async_remote_copy(
            src_ref=buf.at[h, way, k],
            dst_ref=buf.at[h, way, k + 1],
            send_sem=rs.at[stream, h, way, k],
            recv_sem=rr.at[stream, h, way, k],
            device_id={"expert": sides[way]},
            device_id_type=MESH,
        )

    def target(h, way, k):
        ahead_by = hops[h][way] - k
        return lax.rem(me + (ahead_by if way == 0 else ring - ahead_by), ring)

    def begin(stream):
        for h in range(2):
            for way in range(2):
                (red_f, red_b)[stream][h, way, 0] = part(stream, h, target(h, way, 0)).astype(BF16)
                reduce(stream, h, way, 0).start()

    begin(0)
    for h in range(2):
        arrived(1, h, h, half - 1)
    use_b(source(0, half - 1))
    d_hidden = acc_b[...]
    dgu[:units] = (d_hidden * coef_g[...]).astype(BF16)
    dgu[units:] = (d_hidden * coef_u[...]).astype(BF16)
    begin(1)

    def down_piece(g):
        raw = gath_b[pl.ds(GROUP * g, GROUP)].reshape(GROUP * width, rows)
        shards = (raw.astype(F32) * bweight).astype(BF16)
        start = pl.multiple_of(g * (GROUP * width), LANES)
        dg[:, pl.ds(start, GROUP * width)] = dot_t(hbt[...], shards)

    def relay(stream, h, way, k):
        buf = (red_f, red_b)[stream]
        term = part(stream, h, target(h, way, k))
        reduce(stream, h, way, k - 1).wait_recv()
        buf[h, way, k] = (buf[h, way, k].astype(F32) + term).astype(BF16)
        reduce(stream, h, way, k).start()
        gather_copy(stream, h, way, k, me).wait_send()

        @pl.when(k >= 2)
        def _():
            reduce(stream, h, way, k - 2).wait_send()

    def reduce_step(k):
        for stream, h in flows:
            for way in range(2):
                if hops[h][way] == half:
                    relay(stream, h, way, k)
                else:

                    @pl.when(k < half - 1)
                    def _():
                        relay(stream, h, way, k)

    def early(k, carry):
        reduce_step(k)
        down_piece(k - 1)
        return carry

    def late(k, carry):
        reduce_step(k)
        return carry

    def give():
        return pltpu.make_async_remote_copy(
            src_ref=dg.at[pl.ds(pl.multiple_of(peer * (units // 2), 8), units // 2)],
            dst_ref=dg_in,
            send_sem=dp_send,
            recv_sem=dp_recv,
            device_id={"dp": peer},
            device_id_type=MESH,
        )

    mine_rows = pl.ds(pl.multiple_of(replica * (units // 2), 8), units // 2)
    keep = pltpu.make_async_copy(dg_in, dgrad_ref, keep_sem)

    lax.fori_loop(1, groups + 1, early, 0)
    give().start()
    for stream in range(2):
        shift(stream).wait_send()
    for stream, h in flows:
        for way in range(2):
            first(stream, h, way).wait_send()
    lax.fori_loop(groups + 1, half, late, 0)

    give().wait_recv()
    dg_in[...] += dg[mine_rows, :]
    keep.start()

    def deliver(stream, h):
        return pltpu.make_async_copy(
            result.at[stream, band(h)],
            (fout_ref, bout_ref)[stream].at[band(h)],
            out_sem.at[stream, h],
        )

    for stream, h in flows:
        buf = (red_f, red_b)[stream]
        total = part(stream, h, me)
        for way in (1 - h, h):
            last = hops[h][way]
            reduce(stream, h, way, last - 1).wait_recv()
            total = total + buf[h, way, last].astype(F32)
        summed = total.astype(BF16).astype(F32)
        if stream == 0:
            own = gath_f[me, band(h)].astype(F32)
            out = own + fweight_ref[...].astype(F32) * summed
        else:
            out = gath_b[me, band(h)].astype(F32) + summed
        result[stream, band(h)] = out.astype(BF16)
        deliver(stream, h).start()

    give().wait_send()
    keep.wait()
    for stream, h in flows:
        for way in range(2):
            for k in range(max(hops[h][way] - 2, 0), hops[h][way]):
                reduce(stream, h, way, k).wait_send()
    for stream, h in flows:
        deliver(stream, h).wait()


def hand_on(f_ref, b_ref, g_ref, fout_ref, bout_ref, gout_ref, f_held, b_held, g_held, sem, piece_sem):
    pieces = []
    columns = g_ref.shape[1] // 2
    for i in range(g_ref.shape[0] // 8):
        for j in range(2):
            piece = (pl.ds(8 * i, 8), pl.ds(columns * j, columns))
            pieces.append((g_ref.at[piece], g_held.at[piece], gout_ref.at[piece], piece_sem.at[i, j]))
    pieces.append((f_ref, f_held, fout_ref, sem.at[0]))
    pieces.append((b_ref, b_held, bout_ref, sem.at[1]))
    come = [pltpu.make_async_copy(src, held, own.at[0]) for src, held, _, own in pieces]
    go = [pltpu.make_async_copy(held, dst, own.at[1]) for _, held, dst, own in pieces]
    for copy in come:
        copy.start()
    for arrive, leave in zip(come, go):
        arrive.wait()
        leave.start()
    for copy in go:
        copy.wait()


def solution(mesh):
    ring = mesh.shape["expert"]
    sections = mesh.shape["pipe"]
    half = ring // 2

    def body(
        fwd_sent,
        fwd_route,
        fwd_weight,
        bwd_cot,
        bwd_route,
        bwd_weight,
        saved_gate,
        saved_up,
        gate_weight,
        up_weight,
        down_weight,
    ):
        rows, width = fwd_sent.shape[1:]
        units, model = gate_weight.shape[1:]
        dma = pltpu.SemaphoreType.DMA
        hbm = pl.BlockSpec(memory_space=pltpu.HBM)
        capacity = saved_gate.shape[2]
        outs = pl.pallas_call(
            functools.partial(kernel, ring, sections),
            out_shape=(
                jax.ShapeDtypeStruct((width, rows), BF16),
                jax.ShapeDtypeStruct((width, rows), BF16),
                jax.ShapeDtypeStruct((units // 2, model), F32),
            ),
            in_specs=[hbm] * 11,
            out_specs=(hbm,) * 3,
            scratch_shapes=[
                pltpu.VMEM((1, rows), jnp.int32),
                pltpu.VMEM((units, capacity), BF16),
                pltpu.VMEM((units, capacity), BF16),
                pltpu.VMEM((1, rows), BF16),
                pltpu.VMEM((1, rows), jnp.int32),
                pltpu.VMEM((1, rows), BF16),
                pltpu.VMEM((units, model), BF16),
                pltpu.VMEM((units, model), BF16),
                pltpu.VMEM((units, model), BF16),
                pltpu.VMEM((2, width, rows), BF16),
                pltpu.VMEM((ring, width, rows), BF16),
                pltpu.VMEM((ring, width, rows), BF16),
                pltpu.VMEM((2, 2, half + 1, width // 2, rows), BF16),
                pltpu.VMEM((2, 2, half + 1, width // 2, rows), BF16),
                pltpu.VMEM((ring, 2 * units, width), BF16),
                pltpu.VMEM((ring, units, width), BF16),
                pltpu.VMEM((ring, width, 2 * units), BF16),
                pltpu.VMEM((ring, width, units), BF16),
                pltpu.VMEM((2 * units, rows), F32),
                pltpu.VMEM((units, rows), F32),
                pltpu.VMEM((units, rows), F32),
                pltpu.VMEM((units, rows), F32),
                pltpu.VMEM((units, rows), BF16),
                pltpu.VMEM((units, rows), BF16),
                pltpu.VMEM((2 * units, rows), BF16),
                pltpu.VMEM((units, model), F32),
                pltpu.VMEM((units // 2, model), F32),
                dma((9,)),
                dma,
                dma((2, 2)),
                dma((2,)),
                dma((2,)),
            ]
            + [dma((2, 2, 2, half))] * 4
            + [dma, dma],
            compiler_params=pltpu.CompilerParams(
                collective_id=0, has_side_effects=True, vmem_limit_bytes=56 * 1024 * 1024
            ),
        )(
            fwd_sent[0].T,
            fwd_route[0].T,
            fwd_weight[0].T,
            bwd_cot[0].T,
            bwd_route[0].T,
            bwd_weight[0].T,
            saved_gate[0, 0].T,
            saved_up[0, 0].T,
            gate_weight[0],
            up_weight[0],
            down_weight[0],
        )
        outs = pl.pallas_call(
            hand_on,
            out_shape=tuple(jax.ShapeDtypeStruct(out.shape, out.dtype) for out in outs),
            in_specs=[hbm] * 3,
            out_specs=(hbm,) * 3,
            scratch_shapes=[pltpu.VMEM(out.shape, out.dtype) for out in outs]
            + [dma((2, 2)), dma((units // 16, 2, 2))],
        )(*outs)
        return outs[0].T[None], outs[1].T[None], outs[2][None]

    in_specs = (
        P("pipe", "dp", "expert"),
        P("pipe", "dp", None),
        P("pipe", "dp", None),
        P("pipe", "dp", "expert"),
        P("pipe", "dp", None),
        P("pipe", "dp", None),
        P("pipe", "dp", None, "expert"),
        P("pipe", "dp", None, "expert"),
        P("pipe", "expert", None),
        P("pipe", "expert", None),
        P("pipe", "expert", None),
    )
    out_specs = (
        P("pipe", "dp", "expert"),
        P("pipe", "dp", "expert"),
        P("pipe", ("expert", "dp"), None),
    )
    return jax.shard_map(body, mesh=mesh, in_specs=in_specs, out_specs=out_specs, check_vma=False)
```
